32 devices in a mesh: ctx: 4 (over y, x), wa: 8 (over z, core).
Axes of the slice: x: 2, y: 2, z: 4, core: 2. Of those that a mesh axis runs over, the one named last changes fastest.
Arguments:
- block_input: float32 [8, 512, 2048], P('wa', 'ctx'), may hold values from -6 to 6
- query_weight: bfloat16 [2048, 4096], P('wa'), may hold values from -0.125 to 0.125
- key_projection_matrix: bfloat16 [2048, 512], P('wa'), may hold values from -0.125 to 0.125
- value_projection_matrix: bfloat16 [2048, 512], P('wa'), may hold values from -0.125 to 0.125
- output_weight: bfloat16 [4096, 2048], P('wa'), may hold values from -0.1875 to 0.1875
- attention_gain: bfloat16 [2048], P('wa'), may hold values from 0.5 to 1.5
- feedforward_gain: bfloat16 [2048], P('wa'), may hold values from 0.5 to 1.5
- query_gain: bfloat16 [128], P('wa'), may hold values from 0.796875 to 1.296875
- key_gain: bfloat16 [128], P('wa'), may hold values from 0.796875 to 1.296875
- expert_gate: bfloat16 [32, 2048, 768], P(('ctx', 'wa')), may hold values from -0.125 to 0.125
- expert_up: bfloat16 [32, 2048, 768], P(('ctx', 'wa')), may hold values from -0.125 to 0.125
- expert_down: bfloat16 [32, 768, 2048], P(('ctx', 'wa')), may hold values from -0.3125 to 0.3125
- expert_ids: int32 [8, 512, 8], P('wa', 'ctx'), may hold values from 0 to 31, all different within a row; in each aligned block of 128 rows (0 to 127, 128 to 255, ..., all dimensions but the last counted through in order) at most 64 rows name the same one
- route_gates: bfloat16 [8, 512, 8], P('wa', 'ctx'), may hold values from 0.25 to 1
- cotangent: float32 [8, 512, 2048], P('wa', 'ctx'), may hold values from -6 to 6
Outputs:
- block_output: float32 [8, 512, 2048], P('wa', 'ctx')
- input_grad: float32 [8, 512, 2048], P('wa', 'ctx')
- query_weight_grad: float32 [2048, 4096], P('wa')
- key_weight_grad: float32 [2048, 512], P('wa')
- value_weight_grad: float32 [2048, 512], P('wa')
- output_weight_grad: float32 [4096, 2048], P('wa')
- attention_gain_grad: float32 [2048], P('wa')
- feedforward_gain_grad: float32 [2048], P('wa')
- query_gain_grad: float32 [128], P('wa')
- key_gain_grad: float32 [128], P('wa')
- expert_gate_grad: float32 [32, 2048, 768], P(('ctx', 'wa'))
- expert_up_grad: float32 [32, 2048, 768], P(('ctx', 'wa'))
- expert_down_grad: float32 [32, 768, 2048], P(('ctx', 'wa'))
The draws below stay inside these ranges and needn't reach their ends.
Inputs may be any that keep to these rules, and one draw needn't show every extreme that they name: `expert_ids`: each row names 8 different experts; the rows of one sequence block (128 rows in sequence order) name any one expert at most 64 times, a bound that some block reaches.
All inputs are finite; a program needn't handle non-finite values.
Results may differ from the reference program's by a relative error of at most 0.033.
Values may be sent and summed in bfloat16 or wider, within the bound.
No kernel may reach another device: no remote copies, remote signals or barrier semaphores. Data moves between devices by JAX's collectives and lax.ppermute only.
A program may use at most 320 MiB of HBM per device.

```python
import math
import jax
import jax.numpy as jnp
import numpy as np
from jax import lax

MODEL_WIDTH = 2048
QUERY_HEADS = 32
KEY_VALUE_HEADS = 4
HEAD_SIZE = 128
FF = 768
TOP = 8
TOK_DEV = 128
LEN = 512
SEQS = 8
EXPERTS = 32
CAP = 64
N_CTX = 4
N_WA = 8


def levels(rng, shape, pieces, smallest, high):
    loudness, own = 1.0, jax.random.fold_in(rng, 6)
    for dim, shards_of in pieces:
        draws = jnp.exp(jax.random.uniform(jax.random.fold_in(own, dim), (shards_of,), jnp.float32, smallest / len(pieces), high / len(pieces)))
        loudness = loudness * jnp.repeat(draws, shape[dim] // shards_of).reshape([-1 if axis == dim else 1 for axis in range(len(shape))])
    return loudness


def shared_out(rng, own, number, rows, number_of, top, reach, skew):
    order = jax.random.permutation(rng, number_of)
    packed, common = shares(number_of, rows * top, reach, skew, True), shares(number_of, rows * top, reach, skew, False)
    places = jnp.arange(number_of)

    def named(lengths, turn):
        used = int((lengths > 0).sum())
        fixed = max(1, used // 4)
        shifted = fixed + (places - fixed + turn * (used - fixed)) % max(1, number_of - fixed)
        return jnp.zeros((number_of,), jnp.int32).at[order[jnp.where(places < fixed, places, shifted)]].set(jnp.asarray(lengths, jnp.int32))

    lengths = jnp.where(number % 4 == 0, named(packed, number // 4), named(common, number - number // 4 - 1))
    mixed = jax.random.permutation(jax.random.fold_in(own, 3), number_of)
    giver, taker = mixed[0:number_of // 2 * 2:2], mixed[1:number_of // 2 * 2:2]
    margin = jnp.minimum(lengths[giver] - 1, reach - lengths[taker]) // 2
    margin = jnp.where((giver == order[0]) | (taker == order[0]) | (lengths[taker] == 0), 0, jnp.maximum(margin, 0))
    shifted = jax.random.randint(jax.random.fold_in(own, 4), (number_of // 2,), 0, 1 << 20) % (margin + 1)
    lengths = lengths.at[giver].add(-shifted).at[taker].add(shifted)
    members = jnp.searchsorted(jnp.cumsum(lengths), jnp.arange(rows * top), side="right").astype(jnp.int32)
    table = members.reshape(top, rows).T
    table = table[jax.random.permutation(jax.random.fold_in(own, 1), rows)]
    turn = jax.random.randint(jax.random.fold_in(own, 2), (rows, 1), 0, top)
    return jnp.take_along_axis(table, (jnp.arange(top)[None, :] + turn) % top, axis=1)


def shares(number_of, total, reach, lean, full):
    portions = [(1 << 20) // math.isqrt(rank ** lean) + 1 for rank in range(1, number_of + 1)]
    largest = reach if full else min(reach, max(-(-total // number_of), total * portions[0] // sum(portions)))
    least = 1 if total - largest >= number_of - 1 else 0
    holding, spare = [largest] + [least] * (number_of - 1), total - largest - least * (number_of - 1)
    while spare > 0:
        free = [i for i in range(1, number_of) if holding[i] < largest] or [i for i in range(1, number_of) if holding[i] < reach]
        mass, remaining = sum([portions[i] for i in free]), spare
        for i in free:
            more = min(reach - holding[i], max(1, remaining * portions[i] // mass), spare)
            holding[i] = holding[i] + more
            spare = spare - more
    return np.array(holding)


def normal_values(rng, dims, width, limit, split=(), kind=jnp.bfloat16):
    array = jax.random.normal(rng, dims, jnp.float32) * width
    if len(split) > 0:
        array = levels(rng, dims, split, -0.22, 0.18) * array
    return jnp.clip(array, min=-limit, max=limit).astype(kind)


def setup_inputs(seed: int = 0) -> dict:
    key_list = jax.random.split(jax.random.key(seed), 16)
    block_input = normal_values(key_list[0], (SEQS, LEN, MODEL_WIDTH), 1.0, 6.0, ((0, 8), (1, 4)), jnp.float32)
    query_weight = normal_values(key_list[1], (MODEL_WIDTH, QUERY_HEADS * HEAD_SIZE), MODEL_WIDTH ** -0.5, 0.125, ((0, 8),))
    key_projection_matrix = normal_values(key_list[2], (MODEL_WIDTH, KEY_VALUE_HEADS * HEAD_SIZE), MODEL_WIDTH ** -0.5, 0.125, ((0, 8),))
    value_projection_matrix = normal_values(key_list[3], (MODEL_WIDTH, KEY_VALUE_HEADS * HEAD_SIZE), MODEL_WIDTH ** -0.5, 0.125, ((0, 8),))
    output_weight = normal_values(key_list[4], (QUERY_HEADS * HEAD_SIZE, MODEL_WIDTH), (QUERY_HEADS * HEAD_SIZE // 4) ** -0.5, 0.1875, ((0, 8),))
    attention_gain = jnp.clip(1.0 + 0.1 * jax.random.normal(key_list[5], (MODEL_WIDTH,), jnp.float32), 0.5, 1.5).astype(jnp.bfloat16)
    feedforward_gain = jnp.clip(1.0 + 0.1 * jax.random.normal(key_list[6], (MODEL_WIDTH,), jnp.float32), 0.5, 1.5).astype(jnp.bfloat16)
    query_gain = jnp.clip(jnp.exp(math.log(1.296875) - 0.48701498 * jax.random.uniform(key_list[7], (HEAD_SIZE,), jnp.float32) ** levels(key_list[7], (HEAD_SIZE,), ((0, 8),), -0.2, 0.2)), 0.796875, 1.296875).astype(jnp.bfloat16)
    key_gain = jnp.clip(jnp.exp(math.log(1.296875) - 0.48701498 * jax.random.uniform(key_list[8], (HEAD_SIZE,), jnp.float32) ** levels(key_list[8], (HEAD_SIZE,), ((0, 8),), -0.2, 0.2)), 0.796875, 1.296875).astype(jnp.bfloat16)
    expert_gate = normal_values(key_list[9], (EXPERTS, MODEL_WIDTH, FF), MODEL_WIDTH ** -0.5, 0.125, ((0, 32),))
    expert_up = normal_values(key_list[10], (EXPERTS, MODEL_WIDTH, FF), MODEL_WIDTH ** -0.5, 0.125, ((0, 32),))
    expert_down = normal_values(key_list[11], (EXPERTS, FF, MODEL_WIDTH), (FF // 2) ** -0.5, 0.3125, ((0, 32),))
    expert_ids_keys = jax.random.split(jax.random.fold_in(key_list[12], 1), SEQS * LEN // TOK_DEV)
    expert_ids_turns = jax.random.permutation(jax.random.fold_in(key_list[12], 3), SEQS * LEN // TOK_DEV)
    expert_ids = jax.vmap(lambda own, number: shared_out(jax.random.fold_in(key_list[12], 2), own, number, TOK_DEV, EXPERTS, TOP, CAP, 1))(expert_ids_keys, expert_ids_turns).reshape((SEQS, LEN, TOP))
    route_gates = jnp.clip(0.25 + 0.75 * jax.random.uniform(key_list[13], (SEQS, LEN, TOP), jnp.float32) ** levels(key_list[13], (SEQS, LEN, TOP), ((0, 8), (1, 4)), -0.2, 0.2), 0.25, 1.0).astype(jnp.bfloat16)
    cotangent = normal_values(key_list[14], (SEQS, LEN, MODEL_WIDTH), 1.0, 6.0, ((0, 8), (1, 4)), jnp.float32)
    return {"block_input": block_input, "query_weight": query_weight, "key_projection_matrix": key_projection_matrix, "value_projection_matrix": value_projection_matrix, "output_weight": output_weight, "attention_gain": attention_gain, "feedforward_gain": feedforward_gain, "query_gain": query_gain, "key_gain": key_gain, "expert_gate": expert_gate, "expert_up": expert_up, "expert_down": expert_down, "expert_ids": expert_ids, "route_gates": route_gates, "cotangent": cotangent}


EPSILON = 1e-06
ROPE_BASE = 1000000.0

def inv_root(values):
    return lax.rsqrt(lax.optimization_barrier(jnp.mean(values * values, axis=-1, keepdims=True)) + EPSILON)

def rope_tables(positions):
    half_width = HEAD_SIZE // 2
    frequency = ROPE_BASE ** (-(jnp.arange(half_width).astype(positions.dtype) * 2.0 / HEAD_SIZE))
    angles = positions[:, None] * frequency[None, :]
    return (jnp.cos(angles)[:, None, :], jnp.sin(angles)[:, None, :])

def rotate(values, cosine, sine):
    half_width = values.shape[-1] // 2
    first_half = values[..., :half_width]
    second_half = values[..., half_width:]
    return jnp.concatenate([first_half * cosine - second_half * sine, second_half * cosine + first_half * sine], axis=-1)

def unrotate(values, cosine, sine):
    half_width = values.shape[-1] // 2
    first_half = values[..., :half_width]
    second_half = values[..., half_width:]
    return jnp.concatenate([first_half * cosine + second_half * sine, second_half * cosine - first_half * sine], axis=-1)

def round_trip(values):
    return lax.optimization_barrier(values.astype(jnp.bfloat16)).astype(jnp.float32)

def attention_forward(block_rows, query_weight, key_projection_matrix, value_projection_matrix, output_weight, attention_gain, query_gain, key_gain):
    sequence_length = block_rows.shape[0]
    queries_per_group = QUERY_HEADS // KEY_VALUE_HEADS
    score_scale = HEAD_SIZE ** (-0.5)
    positions = jnp.arange(sequence_length, dtype=jnp.int32)
    cosine, sine = rope_tables(positions.astype(jnp.float32))
    root_x = inv_root(block_rows)
    x_hat = block_rows * root_x
    normalized_input = (x_hat * attention_gain.astype(jnp.float32)).astype(jnp.bfloat16)
    query = jnp.dot(normalized_input, query_weight, preferred_element_type=jnp.float32).reshape(sequence_length, QUERY_HEADS, HEAD_SIZE)
    unrotated_key = jnp.dot(normalized_input, key_projection_matrix, preferred_element_type=jnp.float32).reshape(sequence_length, KEY_VALUE_HEADS, HEAD_SIZE)
    value_matrix_rows = jnp.dot(normalized_input, value_projection_matrix, preferred_element_type=jnp.float32).astype(jnp.bfloat16).reshape(sequence_length, KEY_VALUE_HEADS, HEAD_SIZE)
    root_q = inv_root(query)
    q_hat = query * root_q
    root_k = inv_root(unrotated_key)
    k_hat = unrotated_key * root_k
    rotated_query = rotate(q_hat * query_gain.astype(jnp.float32), cosine, sine).astype(jnp.bfloat16)
    k_rot = rotate(k_hat * key_gain.astype(jnp.float32), cosine, sine).astype(jnp.bfloat16)
    grouped_query = rotated_query.reshape(sequence_length, KEY_VALUE_HEADS, queries_per_group, HEAD_SIZE).astype(jnp.float32)
    scores = jnp.einsum('qhgd,khd->hgqk', grouped_query, k_rot.astype(jnp.float32), precision=lax.Precision.HIGHEST) * score_scale
    causal = positions[:, None] >= positions[None, :]
    masked = jnp.where(causal, scores, -jnp.inf)
    running_row_maximum = lax.optimization_barrier(jnp.max(masked, axis=-1, keepdims=True))
    log_total = running_row_maximum + jnp.log(lax.optimization_barrier(jnp.sum(jnp.exp(masked - running_row_maximum), axis=-1, keepdims=True)))
    probabilities = jnp.exp(masked - log_total)
    mixed = jnp.einsum('hgqk,khd->qhgd', round_trip(probabilities), value_matrix_rows.astype(jnp.float32), precision=lax.Precision.HIGHEST)
    attended_output = mixed.astype(jnp.bfloat16).reshape(sequence_length, QUERY_HEADS * HEAD_SIZE)
    hidden = block_rows + jnp.dot(attended_output, output_weight, preferred_element_type=jnp.float32)
    return (hidden, normalized_input, x_hat, root_x, q_hat, root_q, k_hat, root_k, grouped_query, k_rot, value_matrix_rows, probabilities, attended_output, cosine, sine)

def reference(block_input, query_weight, key_projection_matrix, value_projection_matrix, output_weight, attention_gain, feedforward_gain, query_gain, key_gain, expert_gate, expert_up, expert_down, expert_ids, route_gates, cotangent):
    attention_weights = (query_weight, key_projection_matrix, value_projection_matrix, output_weight, attention_gain, query_gain, key_gain)

    def forward_only(block_rows):
        return attention_forward(block_rows, *attention_weights)[0]
    hidden = lax.map(forward_only, block_input)
    flat_hidden = hidden.reshape(-1, MODEL_WIDTH)
    root_h = inv_root(flat_hidden)
    h_hat = flat_hidden * root_h
    ffn_in = (h_hat * feedforward_gain.astype(jnp.float32)).astype(jnp.bfloat16)
    routes = expert_ids.reshape(-1)
    gate_flat = route_gates.reshape(-1).astype(jnp.float32)
    flat_cotangent = cotangent.reshape(-1, MODEL_WIDTH)
    row_limit = N_CTX * N_WA * CAP

    def one_expert(running, inputs):
        mixture, d_ffn = running
        number, gate_w, up_w, down_w = inputs
        hits = routes == number
        picked = jnp.nonzero(hits, size=row_limit, fill_value=0)[0].astype(jnp.int32)
        live = (jnp.arange(row_limit, dtype=jnp.int32) < jnp.sum(hits.astype(jnp.int32))).astype(jnp.float32)
        owners = picked // TOP
        rows_in = jnp.where(live[:, None] > 0.5, ffn_in[owners], jnp.zeros((), jnp.bfloat16))
        gate_pre = jnp.dot(rows_in, gate_w, preferred_element_type=jnp.float32)
        up_pre = jnp.dot(rows_in, up_w, preferred_element_type=jnp.float32)
        sigmoid_gate = jax.nn.sigmoid(gate_pre)
        activated = gate_pre * sigmoid_gate
        middle = (activated * up_pre).astype(jnp.bfloat16)
        produced = jnp.dot(middle, down_w, preferred_element_type=jnp.float32).astype(jnp.bfloat16)
        route_weight = gate_flat[picked] * live
        mixture = mixture.at[owners].add(route_weight[:, None] * produced.astype(jnp.float32))
        down_grad = (route_weight[:, None] * flat_cotangent[owners]).astype(jnp.bfloat16)
        grad_down = jnp.dot(middle.T, down_grad, preferred_element_type=jnp.float32)
        d_middle = jnp.dot(down_grad, down_w.T, preferred_element_type=jnp.float32)
        d_gate_pre = (d_middle * up_pre * sigmoid_gate * (1.0 + gate_pre * (1.0 - sigmoid_gate))).astype(jnp.bfloat16)
        d_up_pre = (d_middle * activated).astype(jnp.bfloat16)
        grad_gate = jnp.dot(rows_in.T, d_gate_pre, preferred_element_type=jnp.float32)
        grad_up = jnp.dot(rows_in.T, d_up_pre, preferred_element_type=jnp.float32)
        d_rows = (jnp.dot(d_gate_pre, gate_w.T, preferred_element_type=jnp.float32) + jnp.dot(d_up_pre, up_w.T, preferred_element_type=jnp.float32)).astype(jnp.bfloat16)
        d_ffn = d_ffn.at[owners].add(d_rows.astype(jnp.float32) * live[:, None])
        return ((mixture, d_ffn), (grad_gate, grad_up, grad_down))
    zero_rows = jnp.zeros(flat_hidden.shape, jnp.float32)
    expert_numbers = jnp.arange(EXPERTS, dtype=jnp.int32)
    (mixture, d_ffn), (expert_gate_grad, expert_up_grad, expert_down_grad) = lax.scan(one_expert, (zero_rows, zero_rows), (expert_numbers, expert_gate, expert_up, expert_down))
    block_output = (flat_hidden + mixture).reshape(block_input.shape)
    feedforward_gain_grad = lax.optimization_barrier(jnp.sum(d_ffn * h_hat, axis=0))
    grad_hat = d_ffn * feedforward_gain.astype(jnp.float32)
    d_hidden = flat_cotangent + root_h * (grad_hat - h_hat * lax.optimization_barrier(jnp.mean(grad_hat * h_hat, axis=-1, keepdims=True)))
    d_hidden = d_hidden.reshape(block_input.shape)
    score_scale = HEAD_SIZE ** (-0.5)
    queries_per_group = QUERY_HEADS // KEY_VALUE_HEADS

    def backward_sequence(running, inputs):
        block_rows, d_hid = inputs
        hidden_rows, normalized_input, x_hat, root_x, q_hat, root_q, k_hat, root_k, grouped_query, k_rot, value_matrix_rows, probabilities, attended_output, cosine, sine = attention_forward(block_rows, *attention_weights)
        sequence_length = block_rows.shape[0]
        d_out = d_hid.astype(jnp.bfloat16)
        grad_output = jnp.dot(attended_output.T, d_out, preferred_element_type=jnp.float32)
        grad_attended_output = jnp.dot(d_out, output_weight.T, preferred_element_type=jnp.float32).astype(jnp.bfloat16)
        grad_attention_per_group = grad_attended_output.reshape(sequence_length, KEY_VALUE_HEADS, queries_per_group, HEAD_SIZE).astype(jnp.float32)
        attention_per_group = attended_output.reshape(sequence_length, KEY_VALUE_HEADS, queries_per_group, HEAD_SIZE).astype(jnp.float32)
        row_delta = lax.optimization_barrier(jnp.sum(grad_attention_per_group * attention_per_group, axis=-1)).transpose(1, 2, 0)
        d_prob = jnp.einsum('qhgd,khd->hgqk', grad_attention_per_group, value_matrix_rows.astype(jnp.float32), precision=lax.Precision.HIGHEST)
        d_scores = probabilities * (d_prob - row_delta[..., None])
        value_gradient = jnp.einsum('hgqk,qhgd->khd', round_trip(probabilities), grad_attention_per_group, precision=lax.Precision.HIGHEST)
        d_round = round_trip(d_scores)
        d_qrot = (jnp.einsum('hgqk,khd->qhgd', d_round, k_rot.astype(jnp.float32), precision=lax.Precision.HIGHEST) * score_scale).reshape(sequence_length, QUERY_HEADS, HEAD_SIZE)
        d_krot = jnp.einsum('hgqk,qhgd->khd', d_round, grouped_query, precision=lax.Precision.HIGHEST) * score_scale
        d_qn = unrotate(d_qrot, cosine, sine)
        d_kn = unrotate(d_krot, cosine, sine)
        grad_qgain = lax.optimization_barrier(jnp.sum(d_qn * q_hat, axis=(0, 1)))
        grad_kgain = lax.optimization_barrier(jnp.sum(d_kn * k_hat, axis=(0, 1)))
        grad_q = d_qn * query_gain.astype(jnp.float32)
        d_query = root_q * (grad_q - q_hat * lax.optimization_barrier(jnp.mean(grad_q * q_hat, axis=-1, keepdims=True)))
        grad_k = d_kn * key_gain.astype(jnp.float32)
        key_gradient = root_k * (grad_k - k_hat * lax.optimization_barrier(jnp.mean(grad_k * k_hat, axis=-1, keepdims=True)))
        d_query_b = d_query.reshape(sequence_length, QUERY_HEADS * HEAD_SIZE).astype(jnp.bfloat16)
        key_gradient_block = key_gradient.reshape(sequence_length, KEY_VALUE_HEADS * HEAD_SIZE).astype(jnp.bfloat16)
        value_gradient_block = value_gradient.reshape(sequence_length, KEY_VALUE_HEADS * HEAD_SIZE).astype(jnp.bfloat16)
        grad_query = jnp.dot(normalized_input.T, d_query_b, preferred_element_type=jnp.float32)
        grad_key = jnp.dot(normalized_input.T, key_gradient_block, preferred_element_type=jnp.float32)
        grad_value = jnp.dot(normalized_input.T, value_gradient_block, preferred_element_type=jnp.float32)
        d_normed = jnp.dot(d_query_b, query_weight.T, preferred_element_type=jnp.float32) + jnp.dot(key_gradient_block, key_projection_matrix.T, preferred_element_type=jnp.float32) + jnp.dot(value_gradient_block, value_projection_matrix.T, preferred_element_type=jnp.float32)
        grad_again = lax.optimization_barrier(jnp.sum(d_normed * x_hat, axis=0))
        grad_n = d_normed * attention_gain.astype(jnp.float32)
        d_rows_in = d_hid + root_x * (grad_n - x_hat * lax.optimization_barrier(jnp.mean(grad_n * x_hat, axis=-1, keepdims=True)))
        sum_q, sum_k, sum_v, sum_o, sum_ag, sum_qg, sum_kg = running
        running = (sum_q + grad_query, sum_k + grad_key, sum_v + grad_value, sum_o + grad_output, sum_ag + grad_again, sum_qg + grad_qgain, sum_kg + grad_kgain)
        return (running, d_rows_in)
    start_sums = (jnp.zeros(query_weight.shape, jnp.float32), jnp.zeros(key_projection_matrix.shape, jnp.float32), jnp.zeros(value_projection_matrix.shape, jnp.float32), jnp.zeros(output_weight.shape, jnp.float32), jnp.zeros((MODEL_WIDTH,), jnp.float32), jnp.zeros((HEAD_SIZE,), jnp.float32), jnp.zeros((HEAD_SIZE,), jnp.float32))
    sums, input_grad = lax.scan(backward_sequence, start_sums, (block_input, d_hidden))
    query_weight_grad, key_weight_grad, value_weight_grad, output_weight_grad, attention_gain_grad, query_gain_grad, key_gain_grad = sums
    return (block_output, input_grad, query_weight_grad, key_weight_grad, value_weight_grad, output_weight_grad, attention_gain_grad, feedforward_gain_grad, query_gain_grad, key_gain_grad, expert_gate_grad, expert_up_grad, expert_down_grad)
```

```python
import jax
import jax.numpy as jnp
from jax import lax
from jax.sharding import PartitionSpec as P

MODEL_WIDTH = 2048
QUERY_HEADS = 32
KEY_VALUE_HEADS = 4
HEAD_SIZE = 128
TOP = 8

EPSILON = 1e-06
ROPE_BASE = 1000000.0
VERY_NEGATIVE = -1e30
EVERY = ("ctx", "wa")


def inv_root(values):
    return lax.rsqrt(jnp.mean(values * values, axis=-1, keepdims=True) + EPSILON)


def rope_tables(positions):
    half_width = HEAD_SIZE // 2
    frequency = ROPE_BASE ** (-(jnp.arange(half_width).astype(positions.dtype) * 2.0 / HEAD_SIZE))
    angles = positions[:, None] * frequency[None, :]
    cosine, sine = jnp.cos(angles), jnp.sin(angles)
    return (
        jnp.concatenate([cosine, cosine], axis=-1),
        jnp.concatenate([-sine, sine], axis=-1),
    )


def swap_halves(values):
    half_width = values.shape[-1] // 2
    return jnp.concatenate([values[..., half_width:], values[..., :half_width]], axis=-1)


def rotate(values, cosine, sine):
    return values * cosine + swap_halves(values) * sine


def unrotate(values, cosine, sine):
    return values * cosine - swap_halves(values) * sine


def dot(a, b, contract):
    return lax.dot_general(a, b, (contract, ((), ())), preferred_element_type=jnp.float32)


def on_device(
    block_input,
    query_weight,
    key_projection_matrix,
    value_projection_matrix,
    output_weight,
    attention_gain,
    feedforward_gain,
    query_gain,
    key_gain,
    expert_gate,
    expert_up,
    expert_down,
    expert_ids,
    route_gates,
    cotangent,
):
    bf16, f32 = jnp.bfloat16, jnp.float32
    n_ctx, n_wa = lax.axis_size("ctx"), lax.axis_size("wa")
    my_ctx, my_wa = lax.axis_index("ctx"), lax.axis_index("wa")
    experts = n_ctx * n_wa
    block_rows = block_input[0]
    rows = block_rows.shape[0]
    length = rows * n_ctx
    capacity = 2 * rows * TOP // experts
    heads = QUERY_HEADS // n_ctx
    per_group = QUERY_HEADS // KEY_VALUE_HEADS
    sharers = per_group // heads
    head_columns = heads * HEAD_SIZE
    out_columns = MODEL_WIDTH // n_ctx
    score_scale = HEAD_SIZE ** (-0.5)

    gains = [attention_gain, feedforward_gain, query_gain, key_gain]
    small = jnp.concatenate(
        [expert_ids[0].astype(bf16).reshape(-1), route_gates[0].reshape(-1)] + gains
    )
    small = lax.all_gather(small, EVERY, axis=0)
    ids_all = small[:, : rows * TOP].reshape(experts, rows, TOP)
    gates_all = small[:, rows * TOP : 2 * rows * TOP].reshape(experts, rows, TOP)
    at = 2 * rows * TOP
    full_gains = []
    for g in gains:
        width = g.shape[0]
        full_gains.append(small[:n_wa, at : at + width].reshape(-1).astype(f32))
        at += width
    gain_attention, gain_feedforward, gain_query, gain_key = full_gains

    group = my_ctx * heads // per_group
    my_query = lax.dynamic_slice_in_dim(query_weight, my_ctx * head_columns, head_columns, 1)
    my_key = lax.dynamic_slice_in_dim(key_projection_matrix, group * HEAD_SIZE, HEAD_SIZE, 1)
    my_value = lax.dynamic_slice_in_dim(value_projection_matrix, group * HEAD_SIZE, HEAD_SIZE, 1)
    my_out = lax.dynamic_slice_in_dim(output_weight, my_ctx * out_columns, out_columns, 1)
    full_qkv = lax.all_gather(
        jnp.concatenate([my_query, my_key, my_value], axis=1), "wa", axis=0, tiled=True
    )
    full_out = lax.all_gather(my_out, "wa", axis=0, tiled=True)

    out_cotangent = cotangent[0]
    cot_all = lax.all_gather(out_cotangent.astype(bf16), EVERY, axis=0)

    root_x = inv_root(block_rows)
    x_hat = block_rows * root_x
    normed = (x_hat * gain_attention).astype(bf16)
    normed_all = lax.all_gather(normed, "ctx", axis=0, tiled=True)
    cosine, sine = rope_tables(jnp.arange(length, dtype=jnp.int32).astype(f32))
    qkv = dot(normed_all, full_qkv, ((1,), (0,)))
    query = qkv[:, :head_columns].reshape(length, heads, HEAD_SIZE).transpose(1, 0, 2)
    key_raw = qkv[:, head_columns : head_columns + HEAD_SIZE]
    value = qkv[:, head_columns + HEAD_SIZE :].astype(bf16)
    root_q = inv_root(query)
    q_hat = query * root_q
    root_k = inv_root(key_raw)
    k_hat = key_raw * root_k
    q_rot = rotate(q_hat * gain_query, cosine, sine).astype(bf16)
    k_rot = rotate(k_hat * gain_key, cosine, sine).astype(bf16)
    positions = jnp.arange(length, dtype=jnp.int32)
    allowed = positions[:, None] >= positions[None, :]
    scores = jnp.einsum("hqd,kd->hqk", q_rot, k_rot, preferred_element_type=f32) * score_scale
    masked = jnp.where(allowed, scores, VERY_NEGATIVE)
    top = jnp.max(masked, axis=-1, keepdims=True)
    weights = jnp.exp(masked - top)
    total = jnp.sum(weights, axis=-1, keepdims=True)
    attended = (
        jnp.einsum("hqk,kd->hqd", weights.astype(bf16), value, preferred_element_type=f32) / total
    ).astype(bf16)
    lse = top + jnp.log(total)
    attended_rows = attended.transpose(1, 0, 2).reshape(length, head_columns)
    attended_all = lax.all_gather(attended_rows, "ctx", axis=0)
    out_part = jnp.einsum(
        "ctk,ckn->tn",
        attended_all,
        full_out.reshape(n_ctx, head_columns, out_columns),
        preferred_element_type=f32,
    ).astype(bf16)
    out_rows = lax.all_to_all(
        out_part.reshape(n_ctx, rows, out_columns), "ctx", split_axis=0, concat_axis=0, tiled=True
    )
    hidden = block_rows + out_rows.transpose(1, 0, 2).reshape(rows, MODEL_WIDTH).astype(f32)

    root_h = inv_root(hidden)
    h_hat = hidden * root_h
    ffn_in = (h_hat * gain_feedforward).astype(bf16)
    ffn_all = lax.all_gather(ffn_in, EVERY, axis=0)
    me = (my_ctx * n_wa + my_wa).astype(bf16)
    mine = ids_all == me
    hit = jnp.any(mine, axis=-1)
    gate_of = jnp.sum(jnp.where(mine, gates_all.astype(f32), 0.0), axis=-1)
    token = jnp.arange(rows, dtype=jnp.int32)
    before = (token[:, None] < token[None, :]).astype(bf16)
    rank = dot(hit.astype(bf16), before, ((1,), (0,))).astype(jnp.int32)
    slot = jnp.arange(capacity, dtype=jnp.int32)
    chosen = (rank[:, None, :] == slot[None, :, None]) & hit[:, None, :]
    pick = chosen.astype(bf16)
    pick_gate = jnp.where(chosen, gate_of[:, None, :], 0.0).astype(bf16)
    gate_w, up_w, down_w = expert_gate[0], expert_up[0], expert_down[0]

    def to_slots(one_hot, values):
        return (
            jnp.einsum("bst,btd->bsd", one_hot, values, preferred_element_type=f32)
            .astype(bf16)
            .reshape(experts * capacity, MODEL_WIDTH)
        )

    def to_tokens(one_hot, values):
        return (
            jnp.einsum(
                "bst,bsd->btd",
                one_hot,
                values.reshape(experts, capacity, MODEL_WIDTH),
                preferred_element_type=f32,
            )
            .astype(bf16)
            .reshape(experts * rows, MODEL_WIDTH)
        )

    down_grad = to_slots(pick_gate, cot_all)
    arrived = to_slots(pick, ffn_all)
    gate_pre = dot(arrived, gate_w, ((1,), (0,)))
    up_pre = dot(arrived, up_w, ((1,), (0,)))
    sigmoid_gate = jax.nn.sigmoid(gate_pre)
    activated = gate_pre * sigmoid_gate
    middle = (activated * up_pre).astype(bf16)
    d_middle = dot(down_grad, down_w, ((1,), (1,)))
    d_gate_pre = (
        d_middle * up_pre * sigmoid_gate * (1.0 + gate_pre * (1.0 - sigmoid_gate))
    ).astype(bf16)
    d_up_pre = (d_middle * activated).astype(bf16)
    d_rows = (
        dot(d_gate_pre, gate_w, ((1,), (1,))) + dot(d_up_pre, up_w, ((1,), (1,)))
    ).astype(bf16)
    d_ffn = lax.psum_scatter(
        to_tokens(pick, d_rows), EVERY, scatter_dimension=0, tiled=True
    ).astype(f32)
    produced = dot(middle, down_w, ((1,), (0,))).astype(bf16)
    mixture = lax.psum_scatter(
        to_tokens(pick_gate, produced), EVERY, scatter_dimension=0, tiled=True
    ).astype(f32)
    block_output = hidden + mixture
    grad_down = dot(middle, down_grad, ((0,), (0,)))
    grad_gate = dot(arrived, d_gate_pre, ((0,), (0,)))
    grad_up = dot(arrived, d_up_pre, ((0,), (0,)))

    grad_feedforward = jnp.sum(d_ffn * h_hat, axis=0)
    grad_hat = d_ffn * gain_feedforward
    d_hidden = out_cotangent + root_h * (
        grad_hat - h_hat * jnp.mean(grad_hat * h_hat, axis=-1, keepdims=True)
    )
    d_out = lax.all_gather(d_hidden.astype(bf16), "ctx", axis=0, tiled=True)
    out_by_rows = lax.all_to_all(
        full_out.reshape(n_ctx, head_columns, out_columns),
        "ctx",
        split_axis=0,
        concat_axis=0,
        tiled=True,
    )
    d_attended = jnp.einsum(
        "tcn,ckn->tk",
        d_out.reshape(length, n_ctx, out_columns),
        out_by_rows,
        preferred_element_type=f32,
    ).astype(bf16)
    d_attended = d_attended.reshape(length, heads, HEAD_SIZE).transpose(1, 0, 2)
    delta = jnp.sum(d_attended.astype(f32) * attended.astype(f32), axis=-1, keepdims=True)
    scores = jnp.einsum("hqd,kd->hqk", q_rot, k_rot, preferred_element_type=f32) * score_scale
    probs = jnp.where(allowed, jnp.exp(scores - lse), 0.0)
    d_prob = jnp.einsum("hqd,kd->hqk", d_attended, value, preferred_element_type=f32)
    d_round = (probs * (d_prob - delta)).astype(bf16)
    d_value = jnp.einsum("hqk,hqd->kd", probs.astype(bf16), d_attended, preferred_element_type=f32)
    d_krot = jnp.einsum("hqk,hqd->kd", d_round, q_rot, preferred_element_type=f32) * score_scale
    d_qrot = jnp.einsum("hqk,kd->hqd", d_round, k_rot, preferred_element_type=f32) * score_scale
    d_qn = unrotate(d_qrot, cosine, sine)
    d_kn = unrotate(d_krot, cosine, sine)
    grad_qgain = jnp.sum(d_qn * q_hat, axis=(0, 1))
    grad_kgain = jnp.sum(d_kn * k_hat, axis=0)
    grad_q = d_qn * gain_query
    d_query = root_q * (grad_q - q_hat * jnp.mean(grad_q * q_hat, axis=-1, keepdims=True))
    grad_k = d_kn * gain_key
    d_key = root_k * (grad_k - k_hat * jnp.mean(grad_k * k_hat, axis=-1, keepdims=True))
    d_query = d_query.astype(bf16).transpose(1, 0, 2).reshape(length, head_columns)
    d_qkv = jnp.concatenate([d_query, d_key.astype(bf16), d_value.astype(bf16)], axis=1)
    d_normed = lax.psum_scatter(
        dot(d_qkv, full_qkv, ((1,), (1,))).astype(bf16), "ctx", scatter_dimension=0, tiled=True
    ).astype(f32)
    grad_attention = jnp.sum(d_normed * x_hat, axis=0)
    grad_n = d_normed * gain_attention
    input_grad = d_hidden + root_x * (
        grad_n - x_hat * jnp.mean(grad_n * x_hat, axis=-1, keepdims=True)
    )

    my_d_out = lax.dynamic_slice_in_dim(d_out, my_ctx * out_columns, out_columns, 1)
    grad_out = jnp.einsum("ctk,tn->ckn", attended_all, my_d_out, preferred_element_type=f32)
    grad_out = lax.psum_scatter(
        grad_out.astype(bf16).reshape(-1, out_columns), "wa", scatter_dimension=0, tiled=True
    )
    grad_out = lax.all_gather(grad_out, "ctx", axis=0)
    grad_out = grad_out.transpose(1, 0, 2).reshape(-1, MODEL_WIDTH).astype(f32)
    grad_qkv = dot(normed_all, d_qkv, ((0,), (0,))).astype(bf16)
    grad_qkv = lax.psum_scatter(grad_qkv, "wa", scatter_dimension=0, tiled=True)
    grad_qkv = lax.all_gather(grad_qkv, "ctx", axis=0).astype(f32)
    share = grad_qkv.shape[1]
    grad_query = (
        grad_qkv[:, :, :head_columns].transpose(1, 0, 2).reshape(share, QUERY_HEADS * HEAD_SIZE)
    )
    by_group = grad_qkv[:, :, head_columns:].reshape(
        KEY_VALUE_HEADS, sharers, share, 2, HEAD_SIZE
    )
    by_group = jnp.sum(by_group, axis=1)
    grad_key = by_group[:, :, 0].transpose(1, 0, 2).reshape(share, KEY_VALUE_HEADS * HEAD_SIZE)
    grad_value = by_group[:, :, 1].transpose(1, 0, 2).reshape(share, KEY_VALUE_HEADS * HEAD_SIZE)
    sums = lax.psum(
        jnp.concatenate([grad_attention, grad_feedforward, grad_qgain, grad_kgain]), EVERY
    )
    gain_grads, at = [], 0
    for g in gains:
        width = g.shape[0]
        gain_grads.append(lax.dynamic_slice_in_dim(sums, at + my_wa * width, width, 0))
        at += width * n_wa
    return (
        block_output[None],
        input_grad[None],
        grad_query,
        grad_key,
        grad_value,
        grad_out,
        *gain_grads,
        grad_gate[None],
        grad_up[None],
        grad_down[None],
    )


def solution(mesh):
    by_row, by_expert = P("wa", None), P(EVERY, None, None)
    tokens = P("wa", "ctx", None)
    gain = P("wa")
    in_specs = (
        (tokens,)
        + (by_row,) * 4
        + (gain,) * 4
        + (by_expert,) * 3
        + (tokens,) * 3
    )
    out_specs = (tokens,) * 2 + (by_row,) * 4 + (gain,) * 4 + (by_expert,) * 3
    return jax.shard_map(
        on_device, mesh=mesh, in_specs=in_specs, out_specs=out_specs, check_vma=False
    )
```

```python
import functools

import jax
import jax.numpy as jnp
from jax import lax
from jax.experimental import pallas as pl
from jax.experimental.pallas import tpu as pltpu
from jax.sharding import PartitionSpec as P

MODEL_WIDTH = 2048
QUERY_HEADS = 32
KEY_VALUE_HEADS = 4
HEAD_SIZE = 128
TOP = 8

EPSILON = 1e-06
ROPE_BASE = 1000000.0
VERY_NEGATIVE = -1e30
EVERY = ("ctx", "wa")
GROUPS = ((1, 3), (0, 2))


def inv_root(values):
    return lax.rsqrt(jnp.mean(values * values, axis=-1, keepdims=True) + EPSILON)


def rope_tables(positions):
    half_width = HEAD_SIZE // 2
    frequency = ROPE_BASE ** (-(jnp.arange(half_width).astype(positions.dtype) * 2.0 / HEAD_SIZE))
    angles = positions[:, None] * frequency[None, :]
    cosine, sine = jnp.cos(angles), jnp.sin(angles)
    return (
        jnp.concatenate([cosine, cosine], axis=-1),
        jnp.concatenate([-sine, sine], axis=-1),
    )


def dot(a, b, contract):
    return lax.dot_general(a, b, (contract, ((), ())), preferred_element_type=jnp.float32)


def add(*terms):
    total = terms[0].astype(jnp.float32)
    for t in terms[1:]:
        total = total + t.astype(jnp.float32)
    return total


def send(values, move):
    n_ctx, n_z = lax.axis_size("ctx"), lax.axis_size("wa") // 2
    pairs = []
    for c in range(n_ctx):
        for z in range(n_z):
            for k in range(2):
                c2, z2, k2 = move(c, z, k)
                pairs.append(((c * n_z + z) * 2 + k, (c2 * n_z + z2 % n_z) * 2 + k2))
    return lax.ppermute(values, EVERY, pairs)


def to_x(values):
    return send(values, lambda c, z, k: (c ^ 1, z, k))


def to_y(values):
    return send(values, lambda c, z, k: (c ^ 2, z, k))


def to_diagonal(values):
    return send(values, lambda c, z, k: (c ^ 3, z, k))


def to_core(values):
    return send(values, lambda c, z, k: (c, z, 1 - k))


def along_z(values, step):
    return send(values, lambda c, z, k: (c, z + step, k))


def after(values, other):
    return values + lax.slice(other, (0,) * other.ndim, (1,) * other.ndim).reshape(()) * 0.0


def hold(values, *others):
    place = pl.BlockSpec(memory_space=pl.ANY)
    return pl.pallas_call(
        lambda *refs: None,
        out_shape=jax.ShapeDtypeStruct(values.shape, values.dtype),
        in_specs=[place] * (1 + len(others)),
        out_specs=place,
        input_output_aliases={0: 0},
        cost_estimate=pl.CostEstimate(flops=0, bytes_accessed=0, transcendentals=0),
        name="hold",
    )(values, *others)


def by_permutes():
    return lax.axis_size("ctx") == 4 and lax.axis_size("wa") == 8


def ctx_order():
    n_ctx = lax.axis_size("ctx")
    if by_permutes():
        return [lax.axis_index("ctx") ^ i for i in range(n_ctx)]
    return [jnp.int32(i) for i in range(n_ctx)]


def ctx_gather(block):
    if not by_permutes():
        return list(lax.all_gather(block, "ctx", axis=0))
    half = block.shape[0] // 2
    x, y = to_x(block), to_y(block)
    first, second = to_y(x[:half]), to_x(y[half:])
    return [block, x, y, jnp.concatenate([first, second])]


def ctx_scatter(blocks):
    if not by_permutes():
        return lax.psum_scatter(
            jnp.concatenate(blocks), "ctx", scatter_dimension=0, tiled=True
        ).astype(jnp.float32)
    o, x, y, d = blocks
    half, kind = o.shape[0] // 2, o.dtype
    from_x = to_x(jnp.concatenate([d[:half], x[:half]]))
    from_y = to_y(jnp.concatenate([d[half:], y[half:]]))
    late_x = to_x(add(x[half:], from_y[:half]).astype(kind))
    late_y = to_y(add(y[:half], from_x[:half]).astype(kind))
    return jnp.concatenate(
        [add(o[:half], from_x[half:], late_y), add(o[half:], from_y[half:], late_x)]
    )


def ctx_exchange(blocks):
    if not by_permutes():
        return list(
            lax.all_to_all(jnp.stack(blocks), "ctx", split_axis=0, concat_axis=0, tiled=True)
        )
    o, x, y, d = blocks
    return [o, to_x(x), to_y(y), to_diagonal(d)]


def scatter_near(mine, other):
    mine = add(mine, to_core(other)).astype(mine.dtype)
    return ctx_scatter(list(mine.reshape(4, -1, mine.shape[2])))


def scatter_far(parts, kind):
    total = None
    for steps, part in zip(GROUPS, parts):
        rows = part.shape[0] // len(steps)
        for i, step in enumerate(steps):
            piece = part[i * rows : (i + 1) * rows]
            if step:
                piece = along_z(piece.astype(kind), -step)
            total = piece if total is None else add(total, piece)
    return total


def scatter_whole(blocks):
    return lax.psum_scatter(
        blocks.reshape(-1, blocks.shape[-1]), EVERY, scatter_dimension=0, tiled=True
    ).astype(jnp.float32)


def block_order():
    n_wa = lax.axis_size("wa")
    if not by_permutes():
        return [(i, w) for i in range(lax.axis_size("ctx")) for w in range(n_wa)]
    w = lax.axis_index("wa")
    z, k = w // 2, w % 2
    return [
        (i, 2 * ((z - step) % 4) + (k ^ b))
        for steps in GROUPS
        for b in range(2)
        for i in range(4)
        for step in steps
    ]


def sum_all(values):
    if not by_permutes():
        return lax.psum(values, EVERY)
    for move in (
        to_core,
        to_x,
        to_y,
        lambda v: send(v, lambda c, z, k: (c, z ^ 1, k)),
        lambda v: send(v, lambda c, z, k: (c, z ^ 2, k)),
    ):
        values = values + move(values)
    return values


def place(parts, order, axis):
    width = parts[0].shape[axis]
    shape = list(parts[0].shape)
    shape[axis] = width * len(parts)
    whole = jnp.zeros(shape, parts[0].dtype)
    for part, where in zip(parts, order):
        whole = lax.dynamic_update_slice_in_dim(whole, part, where * width, axis)
    return whole


def normed_rotated(raw, gain, cosine, sine):
    root = lax.rsqrt(jnp.mean(raw * raw, axis=-1, keepdims=True) + EPSILON)
    hat = raw * root
    scaled = hat * gain
    turned = scaled * cosine + pltpu.roll(scaled, HEAD_SIZE // 2, 1) * sine
    return root, hat, turned.astype(jnp.bfloat16)


def norm_back(d_turned, root, hat, gain, cosine, sine):
    d_scaled = d_turned * cosine - pltpu.roll(d_turned, HEAD_SIZE // 2, 1) * sine
    d_gain = jnp.sum(d_scaled * hat, axis=0, keepdims=True)
    d_hat = d_scaled * gain
    return root * (d_hat - hat * jnp.mean(d_hat * hat, axis=-1, keepdims=True)), d_gain


def softmax_parts(q_rot, k_rot, row_at, column_at):
    scores = dot(q_rot, k_rot, ((1,), (1,))) * HEAD_SIZE ** (-0.5)
    scores = jnp.where(row_at >= column_at, scores, VERY_NEGATIVE)
    weights = jnp.exp(scores - jnp.max(scores, axis=-1, keepdims=True))
    return weights, jnp.sum(weights, axis=-1, keepdims=True)


def attention_kernel(
    q_ref, k_ref, v_ref, gq_ref, gk_ref, cos_ref, sin_ref, row_ref, col_ref, out_ref, k_scratch
):
    @pl.when(pl.program_id(0) == 0)
    def _():
        k_scratch[...] = normed_rotated(k_ref[...], gk_ref[...], cos_ref[...], sin_ref[...])[2]

    _, _, q_rot = normed_rotated(q_ref[...], gq_ref[...], cos_ref[...], sin_ref[...])
    weights, total = softmax_parts(q_rot, k_scratch[...], row_ref[...], col_ref[...])
    value = v_ref[...].astype(jnp.bfloat16)
    mixed = jnp.dot(weights.astype(jnp.bfloat16), value, preferred_element_type=jnp.float32)
    out_ref[...] = (mixed / total).astype(jnp.bfloat16)


def attention_back_kernel(
    q_ref,
    k_ref,
    v_ref,
    gq_ref,
    gk_ref,
    cos_ref,
    sin_ref,
    row_ref,
    col_ref,
    out_ref,
    d_out_ref,
    d_qkv_ref,
    d_gain_ref,
    k_scratch,
    dk_scratch,
    dv_scratch,
):
    bf16 = jnp.bfloat16
    head, heads = pl.program_id(0), pl.num_programs(0)
    scale = HEAD_SIZE ** (-0.5)
    cosine, sine = cos_ref[...], sin_ref[...]

    @pl.when(head == 0)
    def _():
        k_scratch[...] = normed_rotated(k_ref[...], gk_ref[...], cosine, sine)[2]
        dk_scratch[...] = jnp.zeros_like(dk_scratch)
        dv_scratch[...] = jnp.zeros_like(dv_scratch)
        d_gain_ref[...] = jnp.zeros_like(d_gain_ref)

    root, hat, q_rot = normed_rotated(q_ref[...], gq_ref[...], cosine, sine)
    k_rot = k_scratch[...]
    weights, total = softmax_parts(q_rot, k_rot, row_ref[...], col_ref[...])
    probs = weights * (1.0 / total)
    d_out = d_out_ref[...]
    delta = jnp.sum(
        d_out.astype(jnp.float32) * out_ref[...].astype(jnp.float32), axis=-1, keepdims=True
    )
    d_probs = dot(d_out, v_ref[...].astype(bf16), ((1,), (1,)))
    d_scores = (probs * (d_probs - delta)).astype(bf16)
    dv_scratch[...] += dot(probs.astype(bf16), d_out, ((0,), (0,)))
    dk_scratch[...] += dot(d_scores, q_rot, ((0,), (0,))) * scale
    d_turned = jnp.dot(d_scores, k_rot, preferred_element_type=jnp.float32) * scale
    d_raw, d_gain = norm_back(d_turned, root, hat, gq_ref[...], cosine, sine)
    d_qkv_ref[:, pl.ds(pl.multiple_of(head * HEAD_SIZE, HEAD_SIZE), HEAD_SIZE)] = d_raw.astype(bf16)
    d_gain_ref[0:1] += d_gain

    @pl.when(head == heads - 1)
    def _():
        root, hat, _ = normed_rotated(k_ref[...], gk_ref[...], cosine, sine)
        d_raw, d_gain = norm_back(dk_scratch[...], root, hat, gk_ref[...], cosine, sine)
        last = d_qkv_ref.shape[1] - 2 * HEAD_SIZE
        d_qkv_ref[:, last : last + HEAD_SIZE] = d_raw.astype(bf16)
        d_qkv_ref[:, last + HEAD_SIZE :] = dv_scratch[...].astype(bf16)
        d_gain_ref[1:2] = d_gain


def attention_specs(qkv, gain_query, gain_key, cosine, sine, positions):
    length, heads = qkv.shape[0], qkv.shape[1] // HEAD_SIZE - 2

    def column(which):
        return pl.BlockSpec((length, HEAD_SIZE), lambda h: (0, which(h)))

    def whole(array):
        return pl.BlockSpec(array.shape, lambda h: (0, 0))

    tables = (
        gain_query[None, :],
        gain_key[None, :],
        cosine,
        sine,
        positions[:, None],
        positions[None, :],
    )
    specs = [column(lambda h: h), column(lambda h: heads), column(lambda h: heads + 1)]
    return heads, (qkv, qkv, qkv) + tables, specs + [whole(t) for t in tables], column(lambda h: h)


def attend(*arguments):
    heads, arrays, specs, column = attention_specs(*arguments)
    length = arrays[0].shape[0]
    return pl.pallas_call(
        attention_kernel,
        out_shape=jax.ShapeDtypeStruct((length, heads * HEAD_SIZE), jnp.bfloat16),
        grid=(heads,),
        in_specs=specs,
        out_specs=column,
        scratch_shapes=[pltpu.VMEM((length, HEAD_SIZE), jnp.bfloat16)],
        compiler_params=pltpu.CompilerParams(vmem_limit_bytes=40 * 2**20),
        name="attention",
    )(*arrays)


def attend_back(attended, d_attended, *arguments):
    heads, arrays, specs, column = attention_specs(*arguments)
    length = arrays[0].shape[0]
    shared = pltpu.VMEM((length, HEAD_SIZE), jnp.float32)
    return pl.pallas_call(
        attention_back_kernel,
        out_shape=(
            jax.ShapeDtypeStruct(arrays[0].shape, jnp.bfloat16),
            jax.ShapeDtypeStruct((8, HEAD_SIZE), jnp.float32),
        ),
        grid=(heads,),
        in_specs=specs + [column, column],
        out_specs=(
            pl.BlockSpec(arrays[0].shape, lambda h: (0, 0)),
            pl.BlockSpec((8, HEAD_SIZE), lambda h: (0, 0)),
        ),
        scratch_shapes=[pltpu.VMEM((length, HEAD_SIZE), jnp.bfloat16), shared, shared],
        compiler_params=pltpu.CompilerParams(vmem_limit_bytes=48 * 2**20),
        name="attention_back",
    )(*arrays, attended, d_attended)


def picks(place_ref, gate_ref, blocks, capacity, rows):
    slot = lax.broadcasted_iota(jnp.int32, (capacity, rows), 0)
    chosen = [place_ref[i] == slot for i in range(blocks)]
    return (
        [jnp.where(c, 1.0, 0.0).astype(jnp.bfloat16) for c in chosen],
        [jnp.where(c, gate_ref[i], 0.0).astype(jnp.bfloat16) for i, c in enumerate(chosen)],
    )


def forward_kernel(where_ref, *refs, blocks):
    bf16, f32 = jnp.bfloat16, jnp.float32
    tokens, refs = refs[:blocks], refs[blocks:]
    place_ref, gate_ref, gate_w_ref, up_w_ref, down_w_ref = refs[:5]
    arrived_ref, gate_pre_ref, up_pre_ref, middle_ref, back_ref = refs[-5:]
    rows = tokens[0].shape[1]
    capacity = arrived_ref.shape[0] // blocks
    plain, gated = picks(place_ref, gate_ref, blocks, capacity, rows)
    for i in range(blocks):
        arrived_ref[i * capacity : (i + 1) * capacity] = jnp.dot(
            plain[i], tokens[i][0], preferred_element_type=f32
        ).astype(bf16)
    arrived = arrived_ref[...]
    gate_pre = jnp.dot(arrived, gate_w_ref[...], preferred_element_type=f32)
    up_pre = jnp.dot(arrived, up_w_ref[...], preferred_element_type=f32)
    gate_pre_ref[...] = gate_pre
    up_pre_ref[...] = up_pre
    middle = (gate_pre * jax.nn.sigmoid(gate_pre) * up_pre).astype(bf16)
    middle_ref[...] = middle
    produced = jnp.dot(middle, down_w_ref[...], preferred_element_type=f32).astype(bf16)
    for i in range(blocks):
        mine = produced[i * capacity : (i + 1) * capacity]
        back_ref[i] = dot(gated[i], mine, ((0,), (0,))).astype(bf16)


def backward_kernel(where_ref, *refs, blocks):
    bf16, f32 = jnp.bfloat16, jnp.float32
    cots, refs = refs[:blocks], refs[blocks:]
    place_ref, gate_ref, gate_w_ref, up_w_ref, down_w_ref, gate_pre_ref, up_pre_ref = refs[:7]
    down_grad_ref, d_gate_ref, d_up_ref, back_ref = refs[-4:]
    rows = cots[0].shape[1]
    capacity = down_grad_ref.shape[0] // blocks
    plain, gated = picks(place_ref, gate_ref, blocks, capacity, rows)
    for i in range(blocks):
        down_grad_ref[i * capacity : (i + 1) * capacity] = jnp.dot(
            gated[i], cots[i][0], preferred_element_type=f32
        ).astype(bf16)
    d_middle = dot(down_grad_ref[...], down_w_ref[...], ((1,), (1,)))
    gate_pre = gate_pre_ref[...]
    sigmoid_gate = jax.nn.sigmoid(gate_pre)
    d_gate = d_middle * up_pre_ref[...] * sigmoid_gate * (1.0 + gate_pre * (1.0 - sigmoid_gate))
    d_gate = d_gate.astype(bf16)
    d_up = (d_middle * (gate_pre * sigmoid_gate)).astype(bf16)
    d_gate_ref[...] = d_gate
    d_up_ref[...] = d_up
    d_rows = dot(d_gate, gate_w_ref[...], ((1,), (1,))) + dot(d_up, up_w_ref[...], ((1,), (1,)))
    d_rows = d_rows.astype(bf16)
    for i in range(blocks):
        mine = d_rows[i * capacity : (i + 1) * capacity]
        back_ref[i] = dot(plain[i], mine, ((0,), (0,))).astype(bf16)


def over_blocks(kernel, name, blocks, where, place, gate, weights, by_row, widths, waits):
    bf16, f32 = jnp.bfloat16, jnp.float32
    rows, columns = blocks.shape[1:]
    count, step = where.shape[0], 4
    experts, hidden = blocks.shape[0], weights[0].shape[1]
    tall = step * (2 * rows * TOP // experts)
    place_spec = pl.BlockSpec((step, 1, rows), lambda i, w: (i, 0, 0))

    def row_spec(width):
        return pl.BlockSpec((tall, width), lambda i, w: (i, 0))

    results = [jax.ShapeDtypeStruct((count // step * tall, width), t) for width, t in widths]
    return pl.pallas_call(
        functools.partial(kernel, blocks=step),
        out_shape=(*results, jax.ShapeDtypeStruct((count, rows, columns), bf16)),
        grid_spec=pltpu.PrefetchScalarGridSpec(
            num_scalar_prefetch=1,
            grid=(count // step,),
            in_specs=[
                pl.BlockSpec((1, rows, columns), lambda i, w, j=j: (w[i * step + j], 0, 0))
                for j in range(step)
            ]
            + [place_spec, place_spec]
            + [
                pl.BlockSpec(w.shape, lambda i, w: (0, 0), pipeline_mode=pl.Buffered(1))
                for w in weights
            ]
            + [row_spec(r.shape[1]) for r in by_row]
            + [pl.BlockSpec(memory_space=pl.ANY)] * len(waits),
            out_specs=(
                *(row_spec(width) for width, _ in widths),
                pl.BlockSpec((step, rows, columns), lambda i, w: (i, 0, 0)),
            ),
        ),
        compiler_params=pltpu.CompilerParams(vmem_limit_bytes=52 * 2**20),
        cost_estimate=pl.CostEstimate(flops=0, bytes_accessed=0, transcendentals=0),
        name=name,
    )(
        where,
        *([blocks] * step),
        place[:, None, :],
        gate[:, None, :],
        *weights,
        *by_row,
        *waits,
    )


def on_device(
    block_input,
    query_weight,
    key_projection_matrix,
    value_projection_matrix,
    output_weight,
    attention_gain,
    feedforward_gain,
    query_gain,
    key_gain,
    expert_gate,
    expert_up,
    expert_down,
    expert_ids,
    route_gates,
    cotangent,
):
    bf16, f32 = jnp.bfloat16, jnp.float32
    n_ctx, n_wa = lax.axis_size("ctx"), lax.axis_size("wa")
    my_ctx, my_wa = lax.axis_index("ctx"), lax.axis_index("wa")
    experts = n_ctx * n_wa
    block_rows = block_input[0]
    rows = block_rows.shape[0]
    length = rows * n_ctx
    capacity = 2 * rows * TOP // experts
    heads = QUERY_HEADS // n_ctx
    per_group = QUERY_HEADS // KEY_VALUE_HEADS
    sharers = per_group // heads
    head_columns = heads * HEAD_SIZE
    out_columns = MODEL_WIDTH // n_ctx

    order = ctx_order()
    share = query_weight.shape[0]
    gain_rows = attention_gain.astype(f32)[:, None]
    group = my_ctx * heads // per_group

    def tall(values):
        return jnp.pad(values, ((0, share - values.shape[0]), (0, 0)))

    extras = [
        tall(expert_ids[0].astype(bf16)),
        tall(route_gates[0]),
        feedforward_gain[:, None],
        tall(query_gain[:, None]),
        tall(key_gain[:, None]),
    ]
    extras = jnp.concatenate(extras, axis=1)
    extras = jnp.pad(extras, ((0, 0), (0, HEAD_SIZE - extras.shape[1])))
    my_qkv = jnp.concatenate(
        [
            lax.dynamic_slice_in_dim(query_weight, my_ctx * head_columns, head_columns, 1),
            lax.dynamic_slice_in_dim(key_projection_matrix, group * HEAD_SIZE, HEAD_SIZE, 1),
            lax.dynamic_slice_in_dim(value_projection_matrix, group * HEAD_SIZE, HEAD_SIZE, 1),
        ],
        axis=1,
    )
    scaled_qkv = (my_qkv.astype(f32) * gain_rows).astype(bf16)
    packed = lax.all_gather(
        jnp.concatenate([scaled_qkv, extras], axis=1), "wa", axis=0, tiled=True
    )
    full_qkv = packed[:, : head_columns + 2 * HEAD_SIZE]
    extras = packed[:, head_columns + 2 * HEAD_SIZE :].reshape(n_wa, share, HEAD_SIZE)
    at = 2 * TOP
    gain_feedforward, gain_query, gain_key = (
        extras[:, : g.shape[0], at + i].reshape(-1).astype(f32)
        for i, g in enumerate((feedforward_gain, query_gain, key_gain))
    )
    my_out = lax.dynamic_slice_in_dim(output_weight, my_ctx * out_columns, out_columns, 1)
    full_out = lax.all_gather(
        after(my_out.astype(f32), scaled_qkv.astype(f32)).astype(bf16), "wa", axis=0, tiled=True
    )
    root_x = inv_root(block_rows)
    x_hat = block_rows * root_x
    x_all = jnp.concatenate(ctx_gather(x_hat.astype(bf16)))
    out_cotangent = cotangent[0]
    positions = jnp.concatenate([i * rows + jnp.arange(rows, dtype=jnp.int32) for i in order])
    cosine, sine = rope_tables(positions.astype(f32))
    qkv = dot(x_all, full_qkv, ((1,), (0,)))
    arguments = (qkv, gain_query, gain_key, cosine, sine, positions)
    attended_rows = attend(*arguments)
    others = ctx_gather(attended_rows)
    products = [
        dot(
            theirs,
            lax.dynamic_slice_in_dim(full_out, i * head_columns, head_columns, 0),
            ((1,), (0,)),
        ).reshape(n_ctx, rows, out_columns)
        for theirs, i in zip(others, order)
    ]
    seen = [[m ^ i if by_permutes() else m for m in range(n_ctx)] for i in range(n_ctx)]
    out_blocks = ctx_exchange(
        [add(*(p[seen[i][m]] for i, p in enumerate(products))).astype(bf16) for m in range(n_ctx)]
    )
    hidden = block_rows + place(out_blocks, order, 1).astype(f32)
    others = [
        jnp.concatenate([theirs[m * rows : (m + 1) * rows] for m in seen[i]])
        for i, theirs in enumerate(others)
    ]
    attended_all = place(others, order, 1)

    root_h = inv_root(hidden)
    h_hat = hidden * root_h
    ffn_in = (h_hat * gain_feedforward).astype(bf16)
    ffn_all = lax.all_gather(ffn_in, EVERY, axis=0)
    cot_all = lax.all_gather(after(out_cotangent, hidden).astype(bf16), EVERY, axis=0)
    routing = extras[:, :rows].reshape(n_wa * rows, HEAD_SIZE)
    routing = jnp.concatenate(ctx_exchange([routing] * n_ctx)).reshape(experts, rows, HEAD_SIZE)
    places = block_order()
    in_routing = jnp.stack([jnp.int32(i * n_wa + w) for i, w in places])
    in_all = jnp.stack([order[i] * n_wa + w for i, w in places])
    mine = routing[:, :, :TOP] == (my_ctx * n_wa + my_wa).astype(bf16)
    hit = jnp.any(mine, axis=-1)
    gate_of = jnp.sum(jnp.where(mine, routing[:, :, TOP : 2 * TOP].astype(f32), 0.0), axis=-1)
    token = jnp.arange(rows, dtype=jnp.int32)
    before = (token[:, None] < token[None, :]).astype(bf16)
    rank = dot(hit.astype(bf16), before, ((1,), (0,)))
    place_of = jnp.where(hit, rank, -1.0)[in_routing].astype(jnp.int32)
    gate_of = gate_of[in_routing]
    gate_w, up_w, down_w = expert_gate[0], expert_up[0], expert_down[0]

    out_by_rows = lax.all_to_all(
        full_out.reshape(n_ctx, head_columns, out_columns),
        "ctx",
        split_axis=0,
        concat_axis=0,
        tiled=True,
    )
    weights = (gate_w, up_w, down_w)
    hidden_units = gate_w.shape[1]
    sizes = [8 * len(steps) for steps in GROUPS] if by_permutes() else [experts]
    cuts = [slice(sum(sizes[:g]), sum(sizes[: g + 1])) for g in range(len(sizes))]
    forward, produced_parts = [], []
    for cut in cuts:
        *results, back = over_blocks(
            forward_kernel,
            "experts_forward",
            ffn_all,
            in_all[cut],
            place_of[cut],
            gate_of[cut],
            weights,
            (),
            [(MODEL_WIDTH, bf16), (hidden_units, f32), (hidden_units, f32), (hidden_units, bf16)],
            [],
        )
        forward.append(results)
        produced_parts.append(
            scatter_near(*jnp.split(back, 2)) if by_permutes() else scatter_whole(back)
        )
    backward, back_parts = [], []
    for cut, (_, gate_pre, up_pre, _), wait in zip(cuts, forward, produced_parts):
        *results, back = over_blocks(
            backward_kernel,
            "experts_backward",
            cot_all,
            in_all[cut],
            place_of[cut],
            gate_of[cut],
            weights,
            (gate_pre, up_pre),
            [(MODEL_WIDTH, bf16), (hidden_units, bf16), (hidden_units, bf16)],
            [wait, out_by_rows],
        )
        backward.append(results)
        back_parts.append(
            scatter_near(*jnp.split(back, 2)) if by_permutes() else scatter_whole(back)
        )
    if by_permutes():
        mixture, d_ffn = scatter_far(produced_parts, bf16), scatter_far(back_parts, bf16)
    else:
        [mixture], [d_ffn] = produced_parts, back_parts
    block_output = hidden + mixture
    arrived, _, _, middle = (jnp.concatenate(parts) for parts in zip(*forward))
    down_grad, d_gate_pre, d_up_pre = (jnp.concatenate(parts) for parts in zip(*backward))
    grad_down = dot(middle, down_grad, ((0,), (0,)))
    grad_gate = dot(arrived, d_gate_pre, ((0,), (0,)))
    grad_up = dot(arrived, d_up_pre, ((0,), (0,)))

    grad_feedforward = jnp.sum(d_ffn * h_hat, axis=0)
    grad_hat = d_ffn * gain_feedforward
    d_hidden = out_cotangent + root_h * (
        grad_hat - h_hat * jnp.mean(grad_hat * h_hat, axis=-1, keepdims=True)
    )
    d_out = jnp.concatenate(ctx_gather(d_hidden.astype(bf16)))
    d_attended = jnp.einsum(
        "tcn,ckn->tk",
        d_out.reshape(length, n_ctx, out_columns),
        out_by_rows,
        preferred_element_type=f32,
    ).astype(bf16)
    my_d_out = lax.dynamic_slice_in_dim(d_out, my_ctx * out_columns, out_columns, 1)
    grad_out = dot(attended_all, my_d_out, ((0,), (0,))).astype(bf16)
    grad_out = lax.psum_scatter(grad_out, "wa", scatter_dimension=0, tiled=True)
    d_qkv, d_gains = attend_back(attended_rows, d_attended, *arguments)
    grad_qkv = dot(x_all, d_qkv, ((0,), (0,))).astype(bf16)
    grad_qkv = lax.psum_scatter(grad_qkv, "wa", scatter_dimension=0, tiled=True)
    grad_n = dot(d_qkv, full_qkv, ((1,), (1,))).astype(bf16)
    grad_n = ctx_scatter([grad_n[i * rows : (i + 1) * rows] for i in range(n_ctx)])
    input_grad = d_hidden + root_x * (
        grad_n - x_hat * jnp.mean(grad_n * x_hat, axis=-1, keepdims=True)
    )

    grad_out = place(ctx_gather(grad_out), order, 1).astype(f32)
    sums = sum_all(jnp.concatenate([grad_feedforward, d_gains[0], d_gains[1]]))
    parts = ctx_gather(hold(grad_qkv, grad_out, sums, grad_n))
    raw_query = place([p[:, :head_columns] for p in parts], order, 1).astype(f32)
    raw_key, raw_value = (
        jnp.sum(
            place([p[:, a : a + HEAD_SIZE] for p in parts], order, 1)
            .astype(f32)
            .reshape(share, KEY_VALUE_HEADS, sharers, HEAD_SIZE),
            axis=2,
        ).reshape(share, KEY_VALUE_HEADS * HEAD_SIZE)
        for a in (head_columns, head_columns + HEAD_SIZE)
    )
    grad_attention = sum(
        jnp.sum(w.astype(f32) * raw, axis=1)
        for w, raw in (
            (query_weight, raw_query),
            (key_projection_matrix, raw_key),
            (value_projection_matrix, raw_value),
        )
    )
    gain_grads, at = [grad_attention], 0
    for g in (feedforward_gain, query_gain, key_gain):
        width = g.shape[0]
        gain_grads.append(lax.dynamic_slice_in_dim(sums, at + my_wa * width, width, 0))
        at += width * n_wa
    return (
        block_output[None],
        input_grad[None],
        gain_rows * raw_query,
        gain_rows * raw_key,
        gain_rows * raw_value,
        grad_out,
        *gain_grads,
        grad_gate[None],
        grad_up[None],
        grad_down[None],
    )


def solution(mesh):
    by_row, by_expert = P("wa", None), P(EVERY, None, None)
    tokens = P("wa", "ctx", None)
    gain = P("wa")
    in_specs = (
        (tokens,)
        + (by_row,) * 4
        + (gain,) * 4
        + (by_expert,) * 3
        + (tokens,) * 3
    )
    out_specs = (tokens,) * 2 + (by_row,) * 4 + (gain,) * 4 + (by_expert,) * 3
    return jax.shard_map(
        on_device, mesh=mesh, in_specs=in_specs, out_specs=out_specs, check_vma=False
    )
```

```python
import functools

import jax
import jax.numpy as jnp
from jax import lax
from jax.experimental import pallas as pl
from jax.experimental.pallas import tpu as pltpu
from jax.sharding import PartitionSpec as P

MODEL_WIDTH = 2048
QUERY_HEADS = 32
KEY_VALUE_HEADS = 4
HEAD_SIZE = 128
TOP = 8

EPSILON = 1e-06
ROPE_BASE = 1000000.0
VERY_NEGATIVE = -1e30
EVERY = ("ctx", "wa")
GROUPS = ((1, 3), (0, 2))


def inv_root(values):
    return lax.rsqrt(jnp.mean(values * values, axis=-1, keepdims=True) + EPSILON)


def rope_tables(positions):
    half_width = HEAD_SIZE // 2
    frequency = ROPE_BASE ** (-(jnp.arange(half_width).astype(positions.dtype) * 2.0 / HEAD_SIZE))
    angles = positions[:, None] * frequency[None, :]
    cosine, sine = jnp.cos(angles), jnp.sin(angles)
    return (
        jnp.concatenate([cosine, cosine], axis=-1),
        jnp.concatenate([-sine, sine], axis=-1),
    )


def dot(a, b, contract):
    return lax.dot_general(a, b, (contract, ((), ())), preferred_element_type=jnp.float32)


def add(*terms):
    total = terms[0].astype(jnp.float32)
    for t in terms[1:]:
        total = total + t.astype(jnp.float32)
    return total


def send(values, move):
    n_ctx, n_z = lax.axis_size("ctx"), lax.axis_size("wa") // 2
    pairs = []
    for c in range(n_ctx):
        for z in range(n_z):
            for k in range(2):
                c2, z2, k2 = move(c, z, k)
                pairs.append(((c * n_z + z) * 2 + k, (c2 * n_z + z2 % n_z) * 2 + k2))
    return lax.ppermute(values, EVERY, pairs)


def to_x(values):
    return send(values, lambda c, z, k: (c ^ 1, z, k))


def to_y(values):
    return send(values, lambda c, z, k: (c ^ 2, z, k))


def to_diagonal(values):
    return send(values, lambda c, z, k: (c ^ 3, z, k))


def to_core(values):
    return send(values, lambda c, z, k: (c, z, 1 - k))


def along_z(values, step):
    return send(values, lambda c, z, k: (c, z + step, k))


def after(values, other):
    return values + lax.slice(other, (0,) * other.ndim, (1,) * other.ndim).reshape(()) * 0.0


def hold(values, *others):
    place = pl.BlockSpec(memory_space=pl.ANY)
    return pl.pallas_call(
        lambda *refs: None,
        out_shape=jax.ShapeDtypeStruct(values.shape, values.dtype),
        in_specs=[place] * (1 + len(others)),
        out_specs=place,
        input_output_aliases={0: 0},
        cost_estimate=pl.CostEstimate(flops=0, bytes_accessed=0, transcendentals=0),
        name="hold",
    )(values, *others)


def by_permutes():
    return lax.axis_size("ctx") == 4 and lax.axis_size("wa") == 8


def ctx_order():
    n_ctx = lax.axis_size("ctx")
    if by_permutes():
        return [lax.axis_index("ctx") ^ i for i in range(n_ctx)]
    return [jnp.int32(i) for i in range(n_ctx)]


def ctx_gather(block):
    if not by_permutes():
        return list(lax.all_gather(block, "ctx", axis=0))
    half = block.shape[0] // 2
    x, y = to_x(block), to_y(block)
    first, second = to_y(x[:half]), to_x(y[half:])
    return [block, x, y, jnp.concatenate([first, second])]


def ctx_scatter(blocks):
    if not by_permutes():
        return lax.psum_scatter(
            jnp.concatenate(blocks), "ctx", scatter_dimension=0, tiled=True
        ).astype(jnp.float32)
    o, x, y, d = blocks
    half, kind = o.shape[0] // 2, o.dtype
    from_x = to_x(jnp.concatenate([d[:half], x[:half]]))
    from_y = to_y(jnp.concatenate([d[half:], y[half:]]))
    late_x = to_x(add(x[half:], from_y[:half]).astype(kind))
    late_y = to_y(add(y[:half], from_x[:half]).astype(kind))
    return jnp.concatenate(
        [add(o[:half], from_x[half:], late_y), add(o[half:], from_y[half:], late_x)]
    )


def ctx_exchange(blocks):
    if not by_permutes():
        return list(
            lax.all_to_all(jnp.stack(blocks), "ctx", split_axis=0, concat_axis=0, tiled=True)
        )
    o, x, y, d = blocks
    return [o, to_x(x), to_y(y), to_diagonal(d)]


def turn_weights(blocks, order):
    if not by_permutes():
        return list(lax.all_to_all(blocks, "ctx", split_axis=0, concat_axis=0, tiled=True))
    k = lax.axis_index("wa") % 2
    half = blocks.shape[1] // 2
    shape = (1, half, blocks.shape[2])
    mine = [lax.dynamic_slice(blocks, (i, k * half, 0), shape)[0] for i in order[1:]]
    mine = jnp.stack([move(v) for move, v in zip((to_x, to_y, to_diagonal), mine)])
    other = to_core(mine)
    low, high = jnp.where(k == 0, mine, other), jnp.where(k == 0, other, mine)
    own = lax.dynamic_index_in_dim(blocks, order[0], 0)
    return list(jnp.concatenate([own, jnp.concatenate([low, high], axis=1)]))


def gather_groups(block):
    if not by_permutes():
        whole = lax.all_gather(block, EVERY, axis=0)
        return [jnp.split(part, 2) for part in jnp.split(whole, lax.axis_size("ctx"))]
    rows, columns = block.shape
    far = {step: along_z(block, step) if step else block for steps in GROUPS for step in steps}
    groups = []
    for steps in GROUPS:
        mine = jnp.concatenate(ctx_gather(jnp.concatenate([far[step] for step in steps])))
        groups.append([a.reshape(-1, rows, columns) for a in (mine, to_core(mine))])
    return groups


def scatter_near(mine, other):
    mine = add(mine, to_core(other)).astype(mine.dtype)
    return ctx_scatter(list(mine.reshape(4, -1, mine.shape[2])))


def scatter_far(parts, kind):
    total = None
    for steps, part in zip(GROUPS, parts):
        rows = part.shape[0] // len(steps)
        for i, step in enumerate(steps):
            piece = part[i * rows : (i + 1) * rows]
            if step:
                piece = along_z(piece.astype(kind), -step)
            total = piece if total is None else add(total, piece)
    return total


def scatter_near_whole(*blocks):
    blocks = jnp.concatenate(blocks)
    blocks = blocks.reshape(-1, blocks.shape[-1])
    return lax.psum_scatter(blocks, "wa", scatter_dimension=0, tiled=True)


def scatter_far_whole(parts):
    parts = jnp.concatenate(parts)
    return lax.psum_scatter(parts, "ctx", scatter_dimension=0, tiled=True).astype(jnp.float32)


def block_order():
    n_wa = lax.axis_size("wa")
    if not by_permutes():
        return [(i, w) for i in range(lax.axis_size("ctx")) for w in range(n_wa)]
    w = lax.axis_index("wa")
    z, k = w // 2, w % 2
    return [
        (i, 2 * ((z - step) % 4) + (k ^ b))
        for steps in GROUPS
        for b in range(2)
        for i in range(4)
        for step in steps
    ]


def sum_all(values):
    if not by_permutes():
        return lax.psum(values, EVERY)
    for move in (
        to_core,
        to_x,
        to_y,
        lambda v: send(v, lambda c, z, k: (c, z ^ 1, k)),
        lambda v: send(v, lambda c, z, k: (c, z ^ 2, k)),
    ):
        values = values + move(values)
    return values


def place(parts, order, axis):
    width = parts[0].shape[axis]
    shape = list(parts[0].shape)
    shape[axis] = width * len(parts)
    whole = jnp.zeros(shape, parts[0].dtype)
    for part, where in zip(parts, order):
        whole = lax.dynamic_update_slice_in_dim(whole, part, where * width, axis)
    return whole


def normed_rotated(raw, gain, cosine, sine):
    root = lax.rsqrt(jnp.mean(raw * raw, axis=-1, keepdims=True) + EPSILON)
    hat = raw * root
    scaled = hat * gain
    turned = scaled * cosine + pltpu.roll(scaled, HEAD_SIZE // 2, 1) * sine
    return root, hat, turned.astype(jnp.bfloat16)


def norm_back(d_turned, root, hat, gain, cosine, sine):
    d_scaled = d_turned * cosine - pltpu.roll(d_turned, HEAD_SIZE // 2, 1) * sine
    d_gain = jnp.sum(d_scaled * hat, axis=0, keepdims=True)
    d_hat = d_scaled * gain
    return root * (d_hat - hat * jnp.mean(d_hat * hat, axis=-1, keepdims=True)), d_gain


def softmax_parts(q_rot, k_rot, row_at, column_at):
    scores = dot(q_rot, k_rot, ((1,), (1,))) * HEAD_SIZE ** (-0.5)
    scores = jnp.where(row_at >= column_at, scores, VERY_NEGATIVE)
    weights = jnp.exp(scores - jnp.max(scores, axis=-1, keepdims=True))
    return weights, jnp.sum(weights, axis=-1, keepdims=True)


def attention_kernel(
    q_ref, k_ref, v_ref, gq_ref, gk_ref, cos_ref, sin_ref, row_ref, col_ref, out_ref, k_scratch
):
    @pl.when(pl.program_id(0) == 0)
    def _():
        k_scratch[...] = normed_rotated(k_ref[...], gk_ref[...], cos_ref[...], sin_ref[...])[2]

    _, _, q_rot = normed_rotated(q_ref[...], gq_ref[...], cos_ref[...], sin_ref[...])
    weights, total = softmax_parts(q_rot, k_scratch[...], row_ref[...], col_ref[...])
    value = v_ref[...].astype(jnp.bfloat16)
    mixed = jnp.dot(weights.astype(jnp.bfloat16), value, preferred_element_type=jnp.float32)
    out_ref[...] = (mixed / total).astype(jnp.bfloat16)


def attention_back_kernel(
    q_ref,
    k_ref,
    v_ref,
    gq_ref,
    gk_ref,
    cos_ref,
    sin_ref,
    row_ref,
    col_ref,
    out_ref,
    d_out_ref,
    d_qkv_ref,
    d_gain_ref,
    k_scratch,
    dk_scratch,
    dv_scratch,
):
    bf16 = jnp.bfloat16
    head, heads = pl.program_id(0), pl.num_programs(0)
    scale = HEAD_SIZE ** (-0.5)
    cosine, sine = cos_ref[...], sin_ref[...]

    @pl.when(head == 0)
    def _():
        k_scratch[...] = normed_rotated(k_ref[...], gk_ref[...], cosine, sine)[2]
        dk_scratch[...] = jnp.zeros_like(dk_scratch)
        dv_scratch[...] = jnp.zeros_like(dv_scratch)
        d_gain_ref[...] = jnp.zeros_like(d_gain_ref)

    root, hat, q_rot = normed_rotated(q_ref[...], gq_ref[...], cosine, sine)
    k_rot = k_scratch[...]
    weights, total = softmax_parts(q_rot, k_rot, row_ref[...], col_ref[...])
    probs = weights * (1.0 / total)
    d_out = d_out_ref[...]
    delta = jnp.sum(
        d_out.astype(jnp.float32) * out_ref[...].astype(jnp.float32), axis=-1, keepdims=True
    )
    d_probs = dot(d_out, v_ref[...].astype(bf16), ((1,), (1,)))
    d_scores = (probs * (d_probs - delta)).astype(bf16)
    dv_scratch[...] += dot(probs.astype(bf16), d_out, ((0,), (0,)))
    dk_scratch[...] += dot(d_scores, q_rot, ((0,), (0,))) * scale
    d_turned = jnp.dot(d_scores, k_rot, preferred_element_type=jnp.float32) * scale
    d_raw, d_gain = norm_back(d_turned, root, hat, gq_ref[...], cosine, sine)
    d_qkv_ref[:, pl.ds(pl.multiple_of(head * HEAD_SIZE, HEAD_SIZE), HEAD_SIZE)] = d_raw.astype(bf16)
    d_gain_ref[0:1] += d_gain

    @pl.when(head == heads - 1)
    def _():
        root, hat, _ = normed_rotated(k_ref[...], gk_ref[...], cosine, sine)
        d_raw, d_gain = norm_back(dk_scratch[...], root, hat, gk_ref[...], cosine, sine)
        last = d_qkv_ref.shape[1] - 2 * HEAD_SIZE
        d_qkv_ref[:, last : last + HEAD_SIZE] = d_raw.astype(bf16)
        d_qkv_ref[:, last + HEAD_SIZE :] = dv_scratch[...].astype(bf16)
        d_gain_ref[1:2] = d_gain


def attention_specs(qkv, gain_query, gain_key, cosine, sine, positions):
    length, heads = qkv.shape[0], qkv.shape[1] // HEAD_SIZE - 2

    def column(which):
        return pl.BlockSpec((length, HEAD_SIZE), lambda h: (0, which(h)))

    def whole(array):
        return pl.BlockSpec(array.shape, lambda h: (0, 0))

    tables = (
        gain_query[None, :],
        gain_key[None, :],
        cosine,
        sine,
        positions[:, None],
        positions[None, :],
    )
    specs = [column(lambda h: h), column(lambda h: heads), column(lambda h: heads + 1)]
    return heads, (qkv, qkv, qkv) + tables, specs + [whole(t) for t in tables], column(lambda h: h)


def attend(*arguments):
    heads, arrays, specs, column = attention_specs(*arguments)
    length = arrays[0].shape[0]
    return pl.pallas_call(
        attention_kernel,
        out_shape=jax.ShapeDtypeStruct((length, heads * HEAD_SIZE), jnp.bfloat16),
        grid=(heads,),
        in_specs=specs,
        out_specs=column,
        scratch_shapes=[pltpu.VMEM((length, HEAD_SIZE), jnp.bfloat16)],
        compiler_params=pltpu.CompilerParams(vmem_limit_bytes=40 * 2**20),
        name="attention",
    )(*arrays)


def attend_back(attended, d_attended, *arguments):
    heads, arrays, specs, column = attention_specs(*arguments)
    length = arrays[0].shape[0]
    shared = pltpu.VMEM((length, HEAD_SIZE), jnp.float32)
    return pl.pallas_call(
        attention_back_kernel,
        out_shape=(
            jax.ShapeDtypeStruct(arrays[0].shape, jnp.bfloat16),
            jax.ShapeDtypeStruct((8, HEAD_SIZE), jnp.float32),
        ),
        grid=(heads,),
        in_specs=specs + [column, column],
        out_specs=(
            pl.BlockSpec(arrays[0].shape, lambda h: (0, 0)),
            pl.BlockSpec((8, HEAD_SIZE), lambda h: (0, 0)),
        ),
        scratch_shapes=[pltpu.VMEM((length, HEAD_SIZE), jnp.bfloat16), shared, shared],
        compiler_params=pltpu.CompilerParams(vmem_limit_bytes=48 * 2**20),
        name="attention_back",
    )(*arrays, attended, d_attended)


def picks(place_ref, gate_ref, blocks, capacity, rows):
    slot = lax.broadcasted_iota(jnp.int32, (capacity, rows), 0)
    chosen = [place_ref[i] == slot for i in range(blocks)]
    return (
        [jnp.where(c, 1.0, 0.0).astype(jnp.bfloat16) for c in chosen],
        [jnp.where(c, gate_ref[i], 0.0).astype(jnp.bfloat16) for i, c in enumerate(chosen)],
    )


def experts_kernel(where_ref, *refs, blocks):
    bf16, f32 = jnp.bfloat16, jnp.float32
    tokens, refs = refs[:blocks], refs[blocks:]
    cot_ref, late_cot_ref, place_ref, gate_ref, gate_w_ref, up_w_ref, down_w_ref = refs[:7]
    arrived_ref, down_grad_ref, middle_ref, d_gate_ref, d_up_ref = refs[-9:-4]
    rows = tokens[0].shape[1]
    capacity = arrived_ref.shape[0] // blocks
    plain, gated = picks(place_ref, gate_ref, blocks, capacity, rows)
    those = [slice(i * capacity, (i + 1) * capacity) for i in range(blocks)]
    step, steps = pl.program_id(0), pl.num_programs(0)

    def take(cots):
        for i in range(blocks):
            down_grad_ref[those[i]] = jnp.dot(
                gated[i], cots[i], preferred_element_type=f32
            ).astype(bf16)

    pl.when(step < steps // 2)(lambda: take(cot_ref))
    pl.when(step >= steps // 2)(lambda: take(late_cot_ref))
    for i in range(blocks):
        arrived_ref[those[i]] = jnp.dot(
            plain[i], tokens[i][0], preferred_element_type=f32
        ).astype(bf16)
    arrived = arrived_ref[...]
    gate_pre = jnp.dot(arrived, gate_w_ref[...], preferred_element_type=f32)
    up_pre = jnp.dot(arrived, up_w_ref[...], preferred_element_type=f32)
    d_middle = dot(down_grad_ref[...], down_w_ref[...], ((1,), (1,)))
    sigmoid_gate = jax.nn.sigmoid(gate_pre)
    activated = gate_pre * sigmoid_gate
    middle = (activated * up_pre).astype(bf16)
    middle_ref[...] = middle
    d_gate = d_middle * up_pre * sigmoid_gate * (1.0 + gate_pre * (1.0 - sigmoid_gate))
    d_gate = d_gate.astype(bf16)
    d_up = (d_middle * activated).astype(bf16)
    d_gate_ref[...] = d_gate
    d_up_ref[...] = d_up
    d_rows = dot(d_gate, gate_w_ref[...], ((1,), (1,))) + dot(d_up, up_w_ref[...], ((1,), (1,)))
    d_rows = d_rows.astype(bf16)
    produced = jnp.dot(middle, down_w_ref[...], preferred_element_type=f32).astype(bf16)

    def leave(d_rows_ref, produced_ref):
        for i in range(blocks):
            d_rows_ref[i] = dot(plain[i], d_rows[those[i]], ((0,), (0,))).astype(bf16)
            produced_ref[i] = dot(gated[i], produced[those[i]], ((0,), (0,))).astype(bf16)

    pl.when(step < steps // 2)(lambda: leave(refs[-4], refs[-2]))
    pl.when(step >= steps // 2)(lambda: leave(refs[-3], refs[-1]))


def run_experts(tokens, where, cots, place, gate, weights, waits):
    bf16 = jnp.bfloat16
    rows, columns = tokens.shape[1:]
    count, step = where.shape[0], 4
    hidden = weights[0].shape[1]
    tall = step * (2 * rows * TOP // tokens.shape[0])
    steps = count // step
    half = steps // 2

    def block_spec(place):
        return pl.BlockSpec((step, rows, columns), lambda i, w: (place(i), 0, 0))

    place_spec = pl.BlockSpec((step, 1, rows), lambda i, w: (i, 0, 0))
    early = block_spec(lambda i: jnp.minimum(i, half - 1))
    late = block_spec(lambda i: jnp.maximum(i - half, 0))
    widths = (columns, columns, hidden, hidden, hidden)
    return pl.pallas_call(
        functools.partial(experts_kernel, blocks=step),
        out_shape=(
            *(jax.ShapeDtypeStruct((steps * tall, width), bf16) for width in widths),
            *([jax.ShapeDtypeStruct((count // 2, rows, columns), bf16)] * 4),
        ),
        grid_spec=pltpu.PrefetchScalarGridSpec(
            num_scalar_prefetch=1,
            grid=(steps,),
            in_specs=[
                pl.BlockSpec((1, rows, columns), lambda i, w, j=j: (w[i * step + j], 0, 0))
                for j in range(step)
            ]
            + [early, late, place_spec, place_spec]
            + [
                pl.BlockSpec(w.shape, lambda i, w: (0, 0), pipeline_mode=pl.Buffered(1))
                for w in weights
            ]
            + [pl.BlockSpec(memory_space=pl.ANY)] * len(waits),
            out_specs=(
                *(pl.BlockSpec((tall, width), lambda i, w: (i, 0)) for width in widths),
                early,
                late,
                early,
                late,
            ),
        ),
        compiler_params=pltpu.CompilerParams(vmem_limit_bytes=56 * 2**20),
        cost_estimate=pl.CostEstimate(flops=0, bytes_accessed=0, transcendentals=0),
        name="experts",
    )(
        where,
        *([tokens] * step),
        *cots,
        place[:, None, :],
        gate[:, None, :],
        *weights,
        *waits,
    )


def product_kernel(*refs, parts):
    out_ref = refs[-1]
    out_ref[...] = sum(dot(refs[p][...], refs[parts + p][...], ((0,), (0,))) for p in range(parts))


def sum_of_products(left, right, waits):
    parts, tile = len(left), 256
    height, width = left[0].shape[1], right[0].shape[1]
    return pl.pallas_call(
        functools.partial(product_kernel, parts=parts),
        out_shape=jax.ShapeDtypeStruct((height, width), jnp.float32),
        grid=(width // tile,),
        in_specs=[
            pl.BlockSpec(a.shape, lambda i: (0, 0), pipeline_mode=pl.Buffered(1)) for a in left
        ]
        + [pl.BlockSpec((b.shape[0], tile), lambda i: (0, i)) for b in right]
        + [pl.BlockSpec(memory_space=pl.ANY)] * len(waits),
        out_specs=pl.BlockSpec((height, tile), lambda i: (0, i)),
        compiler_params=pltpu.CompilerParams(vmem_limit_bytes=48 * 2**20),
        cost_estimate=pl.CostEstimate(
            flops=2 * sum(a.shape[0] for a in left) * height * width,
            bytes_accessed=4 * height * width,
            transcendentals=0,
        ),
        name="sum_of_products",
    )(*left, *right, *waits)


def on_device(
    block_input,
    query_weight,
    key_projection_matrix,
    value_projection_matrix,
    output_weight,
    attention_gain,
    feedforward_gain,
    query_gain,
    key_gain,
    expert_gate,
    expert_up,
    expert_down,
    expert_ids,
    route_gates,
    cotangent,
):
    bf16, f32 = jnp.bfloat16, jnp.float32
    n_ctx, n_wa = lax.axis_size("ctx"), lax.axis_size("wa")
    my_ctx, my_wa = lax.axis_index("ctx"), lax.axis_index("wa")
    experts = n_ctx * n_wa
    block_rows = block_input[0]
    rows = block_rows.shape[0]
    length = rows * n_ctx
    capacity = 2 * rows * TOP // experts
    heads = QUERY_HEADS // n_ctx
    per_group = QUERY_HEADS // KEY_VALUE_HEADS
    sharers = per_group // heads
    head_columns = heads * HEAD_SIZE
    out_columns = MODEL_WIDTH // n_ctx

    order = ctx_order()
    share = query_weight.shape[0]
    gain_rows = attention_gain.astype(f32)[:, None]
    group = my_ctx * heads // per_group

    def tall(values):
        return jnp.pad(values, ((0, share - values.shape[0]), (0, 0)))

    extras = [
        tall(expert_ids[0].astype(bf16)),
        tall(route_gates[0]),
        feedforward_gain[:, None],
        tall(query_gain[:, None]),
        tall(key_gain[:, None]),
    ]
    extras = jnp.concatenate(extras, axis=1)
    extras = jnp.pad(extras, ((0, 0), (0, HEAD_SIZE - extras.shape[1])))
    my_qkv = jnp.concatenate(
        [
            lax.dynamic_slice_in_dim(query_weight, my_ctx * head_columns, head_columns, 1),
            lax.dynamic_slice_in_dim(key_projection_matrix, group * HEAD_SIZE, HEAD_SIZE, 1),
            lax.dynamic_slice_in_dim(value_projection_matrix, group * HEAD_SIZE, HEAD_SIZE, 1),
        ],
        axis=1,
    )
    scaled_qkv = (my_qkv.astype(f32) * gain_rows).astype(bf16)
    packed = lax.all_gather(
        jnp.concatenate([scaled_qkv, extras], axis=1), "wa", axis=0, tiled=True
    )
    full_qkv = packed[:, : head_columns + 2 * HEAD_SIZE]
    extras = packed[:, head_columns + 2 * HEAD_SIZE :].reshape(n_wa, share, HEAD_SIZE)
    at = 2 * TOP
    gain_feedforward, gain_query, gain_key = (
        extras[:, : g.shape[0], at + i].reshape(-1).astype(f32)
        for i, g in enumerate((feedforward_gain, query_gain, key_gain))
    )
    my_out = lax.dynamic_slice_in_dim(output_weight, my_ctx * out_columns, out_columns, 1)
    full_out = lax.all_gather(
        after(my_out.astype(f32), scaled_qkv.astype(f32)).astype(bf16), "wa", axis=0, tiled=True
    )
    root_x = inv_root(block_rows)
    x_hat = block_rows * root_x
    x_all = jnp.concatenate(ctx_gather(x_hat.astype(bf16)))
    out_cotangent = cotangent[0]
    positions = jnp.concatenate([i * rows + jnp.arange(rows, dtype=jnp.int32) for i in order])
    cosine, sine = rope_tables(positions.astype(f32))
    qkv = dot(x_all, full_qkv, ((1,), (0,)))
    arguments = (qkv, gain_query, gain_key, cosine, sine, positions)
    attended_rows = attend(*arguments)
    others = ctx_gather(attended_rows)
    products = [
        dot(
            theirs,
            lax.dynamic_slice_in_dim(full_out, i * head_columns, head_columns, 0),
            ((1,), (0,)),
        ).reshape(n_ctx, rows, out_columns)
        for theirs, i in zip(others, order)
    ]
    seen = [[m ^ i if by_permutes() else m for m in range(n_ctx)] for i in range(n_ctx)]
    out_blocks = ctx_exchange(
        [add(*(p[seen[i][m]] for i, p in enumerate(products))).astype(bf16) for m in range(n_ctx)]
    )
    hidden = block_rows + place(out_blocks, order, 1).astype(f32)
    others = [
        jnp.concatenate([theirs[m * rows : (m + 1) * rows] for m in seen[i]])
        for i, theirs in enumerate(others)
    ]
    attended_all = place(others, order, 1)

    root_h = inv_root(hidden)
    h_hat = hidden * root_h
    ffn_in = (h_hat * gain_feedforward).astype(bf16)
    ffn_all = lax.all_gather(ffn_in, EVERY, axis=0)
    cot_groups = gather_groups(out_cotangent.astype(bf16))
    routing = extras[:, :rows].reshape(n_wa * rows, HEAD_SIZE)
    routing = jnp.concatenate(ctx_exchange([routing] * n_ctx)).reshape(experts, rows, HEAD_SIZE)
    places = block_order()
    in_routing = jnp.stack([jnp.int32(i * n_wa + w) for i, w in places])
    in_all = jnp.stack([order[i] * n_wa + w for i, w in places])
    mine = routing[:, :, :TOP] == (my_ctx * n_wa + my_wa).astype(bf16)
    hit = jnp.any(mine, axis=-1)
    gate_of = jnp.sum(jnp.where(mine, routing[:, :, TOP : 2 * TOP].astype(f32), 0.0), axis=-1)
    token = jnp.arange(rows, dtype=jnp.int32)
    before = (token[:, None] < token[None, :]).astype(bf16)
    rank = dot(hit.astype(bf16), before, ((1,), (0,)))
    place_of = jnp.where(hit, rank, -1.0)[in_routing].astype(jnp.int32)
    gate_of = gate_of[in_routing]
    gate_w, up_w, down_w = expert_gate[0], expert_up[0], expert_down[0]

    out_by_rows = jnp.stack(turn_weights(full_out.reshape(n_ctx, head_columns, out_columns), order))
    weights = (gate_w, up_w, down_w)
    kept, back_parts, produced, at = [], [], [], 0
    for cots in cot_groups:
        cut = slice(at, at + 2 * cots[0].shape[0])
        at = cut.stop
        *results, back, back_other, forth, forth_other = run_experts(
            ffn_all,
            in_all[cut],
            cots,
            place_of[cut],
            gate_of[cut],
            weights,
            kept[-1][:1] if kept else [],
        )
        kept.append(results)
        if by_permutes():
            if cut.stop == experts:
                back = hold(back, out_by_rows)
            back_parts.append(scatter_near(back, back_other))
        else:
            back_parts.append(scatter_near_whole(back, back_other))
            forth = scatter_near_whole(forth, forth_other)
        produced.append((forth, forth_other))
    if by_permutes():
        d_ffn = scatter_far(back_parts, bf16)
        mixture = scatter_far([scatter_near(hold(a, d_ffn), b) for a, b in produced], bf16)
    else:
        d_ffn = scatter_far_whole(back_parts)
        mixture = scatter_far_whole([forth for forth, _ in produced])
    block_output = hidden + mixture
    grad_feedforward = jnp.sum(d_ffn * h_hat, axis=0)
    grad_hat = d_ffn * gain_feedforward
    d_hidden = out_cotangent + root_h * (
        grad_hat - h_hat * jnp.mean(grad_hat * h_hat, axis=-1, keepdims=True)
    )
    d_out = jnp.concatenate(ctx_gather(d_hidden.astype(bf16)))
    d_attended = add(
        *(
            dot(
                lax.dynamic_slice_in_dim(d_out, where * out_columns, out_columns, 1),
                out_by_rows[i],
                ((1,), (1,)),
            )
            for i, where in enumerate(order)
        )
    ).astype(bf16)
    my_d_out = lax.dynamic_slice_in_dim(d_out, my_ctx * out_columns, out_columns, 1)
    grad_out = dot(attended_all, my_d_out, ((0,), (0,))).astype(bf16)
    grad_out = lax.psum_scatter(grad_out, "wa", scatter_dimension=0, tiled=True)
    d_qkv, d_gains = attend_back(attended_rows, d_attended, *arguments)
    grad_qkv = dot(x_all, d_qkv, ((0,), (0,))).astype(bf16)
    whole_qkv = grad_qkv
    grad_qkv = lax.psum_scatter(grad_qkv, "wa", scatter_dimension=0, tiled=True)
    grad_n = dot(d_qkv, full_qkv, ((1,), (1,))).astype(bf16)
    grad_n = ctx_scatter([grad_n[i * rows : (i + 1) * rows] for i in range(n_ctx)])
    input_grad = d_hidden + root_x * (
        grad_n - x_hat * jnp.mean(grad_n * x_hat, axis=-1, keepdims=True)
    )

    parts = ctx_gather(grad_out)
    arrived, down_grad, middle, d_gate_pre, d_up_pre = zip(*kept)
    grad_down = sum_of_products(middle, down_grad, [whole_qkv])
    grad_gate = sum_of_products(arrived, d_gate_pre, [whole_qkv])
    grad_up = sum_of_products(arrived, d_up_pre, [whole_qkv])
    grad_out = place(parts, order, 1).astype(f32)
    sums = sum_all(jnp.concatenate([grad_feedforward, d_gains[0], d_gains[1]]))
    parts = ctx_gather(grad_qkv)
    raw_query = place([p[:, :head_columns] for p in parts], order, 1).astype(f32)
    raw_key, raw_value = (
        jnp.sum(
            place([p[:, a : a + HEAD_SIZE] for p in parts], order, 1)
            .astype(f32)
            .reshape(share, KEY_VALUE_HEADS, sharers, HEAD_SIZE),
            axis=2,
        ).reshape(share, KEY_VALUE_HEADS * HEAD_SIZE)
        for a in (head_columns, head_columns + HEAD_SIZE)
    )
    grad_attention = sum(
        jnp.sum(w.astype(f32) * raw, axis=1)
        for w, raw in (
            (query_weight, raw_query),
            (key_projection_matrix, raw_key),
            (value_projection_matrix, raw_value),
        )
    )
    gain_grads, at = [grad_attention], 0
    for g in (feedforward_gain, query_gain, key_gain):
        width = g.shape[0]
        gain_grads.append(lax.dynamic_slice_in_dim(sums, at + my_wa * width, width, 0))
        at += width * n_wa
    return (
        block_output[None],
        input_grad[None],
        gain_rows * raw_query,
        gain_rows * raw_key,
        gain_rows * raw_value,
        grad_out,
        *gain_grads,
        grad_gate[None],
        grad_up[None],
        grad_down[None],
    )


def solution(mesh):
    by_row, by_expert = P("wa", None), P(EVERY, None, None)
    tokens = P("wa", "ctx", None)
    gain = P("wa")
    in_specs = (
        (tokens,)
        + (by_row,) * 4
        + (gain,) * 4
        + (by_expert,) * 3
        + (tokens,) * 3
    )
    out_specs = (tokens,) * 2 + (by_row,) * 4 + (gain,) * 4 + (by_expert,) * 3
    return jax.shard_map(
        on_device, mesh=mesh, in_specs=in_specs, out_specs=out_specs, check_vma=False
    )
```
